256 devices in a mesh: section: 8 (over z_hi, core), ctx: 32 (over y, z_lo, x).
Axes of the slice: x: 4, y: 4, z: 8 (z_hi: 4, z_lo: 2; z = z_hi * 2 + z_lo), core: 2. Of those that a mesh axis runs over, the one named last changes fastest.
Arguments:
- queries: bfloat16 [8, 4096, 2560], P('section', 'ctx'), may hold values from -150 to 150
- attn_out: bfloat16 [8, 4096, 2560], P('section', 'ctx'), may hold values from -6 to 6
- grad_out: bfloat16 [8, 4096, 2560], P('section', 'ctx'), may hold values from -6 to 6
- shared_kv: bfloat16 [4096, 1024], P('ctx', 'section'), may hold values from -7 to 7
- ret_query: bfloat16 [4096, 512], P('ctx'), may hold values from -6 to 6
- ret_key: bfloat16 [4096, 512], P('ctx'), may hold values from -6 to 6
- ret_value: bfloat16 [4096, 1024], P('ctx', 'section'), may hold values from -6 to 6
- log_decay: float32 [4096, 4], P('ctx'), may hold values from -0.8 to 0, as said below
Outputs:
- d_queries: bfloat16 [8, 4096, 2560], P('section', 'ctx')
- d_ret_query: float32 [4096, 512], P('ctx')
- d_ret_key: float32 [4096, 512], P('ctx')
- d_ret_value: float32 [4096, 1024], P('ctx', 'section')
- d_log_decay: float32 [4096, 4], P('ctx')
The draws below stay inside these ranges and needn't reach their ends.
Inputs may be any that keep to these rules, and one draw needn't show every extreme that they name: `log_decay`: every entry is negative.
All inputs are finite; a program needn't handle non-finite values.
Results may differ from the reference program's by a relative error of at most 0.0064.
Values may be sent and summed in bfloat16 or wider, within the bound.
No kernel may reach another device: no remote copies, remote signals or barrier semaphores. Data moves between devices by JAX's collectives and lax.ppermute only.
A program may use at most 128 MiB of HBM per device.

```python
import math
import jax
import jax.numpy as jnp
from jax import lax

TOK_DEV = 128
QH = 20
KVH = 4
HD = 128
TOKEN_COUNT = 4096
LAYERS = 8


def shared_pairs(key, pair_count, row_spread):
    base_key, scale_key, pair_key = jax.random.split(key, 3)
    values = jnp.clip(jax.random.normal(base_key, (TOKEN_COUNT, KVH * 2 * HD), jnp.float32), -3.5, 3.5)
    log_spread = math.log(row_spread)
    row_scale = jnp.exp(jax.random.uniform(scale_key, (TOKEN_COUNT, 1), jnp.float32, -1.0, 1.0) * log_spread)
    values = values * row_scale
    records = []
    for pair_index in range(pair_count):
        keys_now = jax.random.split(jax.random.fold_in(pair_key, pair_index), 4)
        query_row = jax.random.randint(keys_now[0], (), TOKEN_COUNT // 2, TOKEN_COUNT)
        first_key = jax.random.randint(keys_now[1], (), 0, query_row + 1)
        second_key = (first_key + 1 + jax.random.randint(keys_now[2], (), 0, query_row)) % (query_row + 1)
        score_gap = jax.random.uniform(keys_now[3], (), jnp.float32, 1.0, 3.0)
        target = 110.0 + 40.0 * (pair_index % 6)
        source = values[first_key].reshape(KVH, 2, HD)
        moved_row = values[second_key].reshape(KVH, 2, HD)
        moved_row = moved_row.at[:, 0].set(source[:, 0] * (1.0 - score_gap / target))
        values = values.at[second_key].set(moved_row.reshape(-1))
        records.append((pair_index % LAYERS, query_row, first_key, target))
    return values


def draw_shared_kv(key, part):
    values = shared_pairs(key, 0, 2.0)
    return values.astype(jnp.bfloat16)


def draw_queries(key, part):
    key = jax.random.fold_in(key, 7)
    noise_key, scale_key = jax.random.split(key)
    result = jnp.clip(jax.random.normal(noise_key, (LAYERS, TOKEN_COUNT, QH * HD), jnp.float32), -3.5, 3.5)
    row_scale = jnp.exp(jax.random.uniform(scale_key, (LAYERS, TOKEN_COUNT, 1), jnp.float32, math.log(0.3), math.log(3.0)))
    result = result * row_scale
    return result.astype(jnp.bfloat16)


def draw_log_decay(key, part):
    key = jax.random.fold_in(key, 11)
    arrangement_seed, quick_seed_handle, gradual_seed_handle, accelerator_seed, iteration_seed, spike_seed_handle, survival_seed = jax.random.split(key, 7)
    head_order = jax.random.permutation(arrangement_seed, KVH)
    fast_count = KVH // 2
    is_fast = head_order < fast_count
    fast_rate = 3.0 / TOK_DEV * jnp.exp(jax.random.uniform(quick_seed_handle, (KVH,), jnp.float32, math.log(0.7), math.log(1.4)))
    slow_rate = 0.25 / TOKEN_COUNT * jnp.exp(jax.random.uniform(gradual_seed_handle, (KVH,), jnp.float32, math.log(0.5), math.log(1.5)))
    head_rate = jnp.where(is_fast, fast_rate, slow_rate)
    device_factor = jnp.exp(jax.random.uniform(accelerator_seed, (TOKEN_COUNT // TOK_DEV, 1, KVH), jnp.float32, math.log(0.6), math.log(1.3)))
    step_factor = jnp.exp(jax.random.uniform(iteration_seed, (TOKEN_COUNT // TOK_DEV, TOK_DEV, KVH), jnp.float32, math.log(0.5), math.log(2.0)))
    log_decay_speeds = -(head_rate * device_factor * step_factor).reshape(TOKEN_COUNT, KVH)
    spike_location = jax.random.randint(spike_seed_handle, (2,), 0, TOKEN_COUNT)
    spike_agrees = jnp.any(jnp.arange(TOKEN_COUNT)[:, None] == spike_location[None, :], axis=1)
    retained_proportion = jax.random.uniform(survival_seed, (KVH,), jnp.float32, 0.5, 0.8)
    log_decay_speeds = log_decay_speeds + jnp.where(spike_agrees[:, None], jnp.log(retained_proportion)[None, :], 0.0)
    return jnp.maximum(log_decay_speeds, -0.8)


def levels(rng, dims, cuts, smallest, largest):
    factor_of = 1.0
    for dim, blocks in cuts:
        heights = jax.random.uniform(jax.random.fold_in(jax.random.fold_in(rng, 6), dim), (blocks,), jnp.float32, smallest / len(cuts), largest / len(cuts))
        factor_of = factor_of * jnp.repeat(jnp.exp(heights), dims[dim] // blocks).reshape((-1,) + (1,) * (len(dims) - 1 - dim))
    return factor_of


def scatter_about(key, extent, deviation, limit, cuts=(), held_as=jnp.bfloat16):
    values = deviation * jax.random.normal(key, extent, jnp.float32)
    if cuts:
        values = values * levels(key, extent, cuts, -0.22, 0.18)
    return jnp.clip(values, -limit, limit).astype(held_as)


def setup_inputs(seed: int = 0) -> dict:
    streams_of = jax.random.split(jax.random.key(seed), 9)
    queries = draw_queries(jax.random.fold_in(streams_of[8], 71), 0)
    attn_out = scatter_about(streams_of[1], (LAYERS, TOKEN_COUNT, QH * HD), 1.0, 6.0, ((0, 8), (1, 32)))
    grad_out = scatter_about(streams_of[2], (LAYERS, TOKEN_COUNT, QH * HD), 1.0, 6.0, ((0, 8), (1, 32)))
    shared_kv = draw_shared_kv(jax.random.fold_in(streams_of[8], 71), 0)
    ret_query = scatter_about(streams_of[4], (TOKEN_COUNT, KVH * HD), 1.0, 6.0, ((0, 32),))
    ret_key = scatter_about(streams_of[5], (TOKEN_COUNT, KVH * HD), 1.0, 6.0, ((0, 32),))
    ret_value = scatter_about(streams_of[6], (TOKEN_COUNT, 2 * KVH * HD), 1.0, 6.0, ((0, 32), (1, 8)))
    log_decay = draw_log_decay(jax.random.fold_in(streams_of[8], 71), 0)
    return {"queries": queries, "attn_out": attn_out, "grad_out": grad_out, "shared_kv": shared_kv, "ret_query": ret_query, "ret_key": ret_key, "ret_value": ret_value, "log_decay": log_decay}


exact_variant = lax.Precision.HIGHEST

def norm_backward(retained, d_shared, head_size):
    row_count = retained.shape[0]
    grouped = retained.reshape(row_count, -1, head_size)
    upstream = d_shared.reshape(row_count, -1, head_size)
    inverse = lax.rsqrt(lax.optimization_barrier(jnp.mean(grouped * grouped, axis=-1, keepdims=True)) + 1e-06)
    normed = grouped * inverse
    result = (upstream - normed * lax.optimization_barrier(jnp.mean(normed * upstream, axis=-1, keepdims=True))) * inverse
    return result.reshape(retained.shape)

def retention_full(query_in, key_in, value_in, decay_in):
    block_count = TOKEN_COUNT // TOK_DEV
    scaled = (query_in * HD ** (-0.5)).reshape(block_count, TOK_DEV, KVH, HD)
    key_blocks = key_in.reshape(block_count, TOK_DEV, KVH, HD)
    value_blocks = value_in.reshape(block_count, TOK_DEV, KVH, 2 * HD)
    decay_blocks = decay_in.reshape(block_count, TOK_DEV, KVH)
    lower_tri = jnp.arange(TOK_DEV)[:, None] >= jnp.arange(TOK_DEV)[None, :]

    def advance(state_now, inputs):
        q_blk, k_blk, v_blk, a_blk = inputs
        cumulative = jnp.cumsum(a_blk, axis=0)
        decay_total = cumulative[-1]
        spread = jnp.where(lower_tri[:, :, None], cumulative[:, None, :] - cumulative[None, :, :], -jnp.inf)
        inner_prod = jnp.einsum('thd,shd->hts', q_blk, k_blk, precision=exact_variant) * jnp.exp(spread).transpose(2, 0, 1)
        outputs = jnp.einsum('hts,shc->thc', inner_prod, v_blk, precision=exact_variant)
        outputs = outputs + jnp.einsum('thd,hdc->thc', q_blk * jnp.exp(cumulative)[:, :, None], state_now, precision=exact_variant)
        local_state = jnp.einsum('thd,thc->hdc', k_blk * jnp.exp(decay_total - cumulative)[:, :, None], v_blk, precision=exact_variant)
        return (jnp.exp(decay_total)[:, None, None] * state_now + local_state, outputs)
    start_state = jnp.zeros((KVH, HD, 2 * HD), jnp.float32)
    _, outputs = lax.scan(advance, start_state, (scaled, key_blocks, value_blocks, decay_blocks))
    return outputs.reshape(TOKEN_COUNT, KVH * 2 * HD)

def reference(queries, attn_out, grad_out, shared_kv, ret_query, ret_key, ret_value, log_decay):
    q_group = QH // KVH
    scaling = HD ** (-0.5)
    paired = shared_kv.astype(jnp.float32).reshape(TOKEN_COUNT, KVH, 2, HD)
    key_all = paired[:, :, 0]
    value_all = paired[:, :, 1]
    key_pos = jnp.arange(TOKEN_COUNT, dtype=jnp.int32)
    block_count = TOKEN_COUNT // TOK_DEV
    zero_index = jnp.zeros((), jnp.int32)

    def attend(grad_sum, flat_index):
        layer_index = (flat_index // block_count).astype(jnp.int32)
        first_row = (flat_index % block_count * TOK_DEV).astype(jnp.int32)

        def take_rows(source_array):
            picked = lax.dynamic_slice(source_array, (layer_index, first_row, zero_index), (1, TOK_DEV, QH * HD))[0]
            return picked.astype(jnp.float32).reshape(TOK_DEV, KVH, q_group, HD)
        q_rows = take_rows(queries)
        gate_rows = take_rows(grad_out)
        output_rows = take_rows(attn_out)
        positions = first_row + jnp.arange(TOK_DEV, dtype=jnp.int32)
        is_valid = key_pos[None, :] <= positions[:, None]
        raw_scores = jnp.einsum('tgrd,kgd->grtk', q_rows, key_all, precision=exact_variant) * scaling
        masked = jnp.where(is_valid, raw_scores, -jnp.inf)
        row_max = lax.optimization_barrier(jnp.max(masked, axis=-1, keepdims=True))
        lse_rows = row_max + jnp.log(lax.optimization_barrier(jnp.sum(jnp.exp(masked - row_max), axis=-1, keepdims=True)))
        weights = jnp.exp(masked - lse_rows)
        weights_b = lax.optimization_barrier(weights.astype(jnp.bfloat16)).astype(jnp.float32)
        output_change = jnp.einsum('xbcu,xbcu->bcx', gate_rows, output_rows, precision=exact_variant)
        d_weight = jnp.einsum('tgrd,kgd->grtk', gate_rows, value_all, precision=exact_variant)
        d_score = (weights * (d_weight - output_change[..., None])).astype(jnp.bfloat16)
        d_score = lax.optimization_barrier(d_score).astype(jnp.float32)
        d_query = (jnp.einsum('grtk,kgd->tgrd', d_score, key_all, precision=exact_variant) * scaling).astype(jnp.bfloat16)
        d_keys = (jnp.einsum('grtk,tgrd->kgd', d_score, q_rows, precision=exact_variant) * scaling).astype(jnp.bfloat16)
        d_values = jnp.einsum('grtk,tgrd->kgd', weights_b, gate_rows, precision=exact_variant).astype(jnp.bfloat16)
        block_terms = jnp.stack([d_keys, d_values], axis=2).reshape(TOKEN_COUNT, 2 * KVH * HD).astype(jnp.float32)
        return (grad_sum + block_terms, d_query.reshape(TOK_DEV, QH * HD))
    start_sum = jnp.zeros((TOKEN_COUNT, 2 * KVH * HD), jnp.float32)
    d_shared, d_rows = lax.scan(attend, start_sum, jnp.arange(LAYERS * block_count, dtype=jnp.int32))
    d_queries = d_rows.reshape(LAYERS, TOKEN_COUNT, QH * HD)
    retained, pullback = jax.vjp(retention_full, ret_query.astype(jnp.float32), ret_key.astype(jnp.float32), ret_value.astype(jnp.float32), log_decay)
    d_retained = norm_backward(retained, d_shared, HD)
    d_query, d_key, d_value, d_decay = pullback(d_retained)
    return (d_queries, d_query, d_key, d_value, d_decay)
```

```python
import functools
import math

import jax
import jax.numpy as jnp
from jax import lax
from jax.experimental import pallas as pl
from jax.experimental.pallas import tpu as pltpu
from jax.sharding import Mesh, PartitionSpec as P

bf16 = jnp.bfloat16
f32 = jnp.float32
EXACT = lax.Precision.HIGHEST
TOK = 128
HD = 128
GROUP = 5
WIDE = GROUP * HD
EXTRA = 16
BLOCKS = 32
SCALE = HD**-0.5
LOG2E = math.log2(math.e)
CTX = ("y", "zlo", "x")
VMEM = pl.BlockSpec(memory_space=pltpu.VMEM)
SMEM = pl.BlockSpec(memory_space=pltpu.SMEM)


ANY = pl.BlockSpec(memory_space=pl.ANY)


def in_hbm(x):
    return pltpu.with_memory_space_constraint(x, pltpu.HBM)


def loaded(kernel, inputs, outputs, *refs):
    ids, far, rest = refs[0], refs[1 : 1 + inputs], refs[1 + inputs :]
    results, near, scratch = rest[:outputs], rest[outputs : outputs + inputs], rest[outputs + inputs : -1]
    copies = [pltpu.make_async_copy(f, n, rest[-1].at[i]) for i, (f, n) in enumerate(zip(far, near))]
    for copy in copies:
        copy.start()
    for copy in copies:
        copy.wait()
    kernel(ids, *near, *results, *scratch)


def call(kernel, outs, args, name, loose=0, scratch=(), limit=8, flops=0, nbytes=0, free=()):
    cost = None
    if flops:
        cost = pl.CostEstimate(flops=flops, bytes_accessed=nbytes, transcendentals=0)
    inputs = [x if i < loose else in_hbm(x) for i, x in enumerate(args[1:])]
    near = [pltpu.VMEM(x.shape, x.dtype) for x in inputs]
    return pl.pallas_call(
        functools.partial(loaded, kernel, len(inputs), len(outs)),
        out_shape=[jax.ShapeDtypeStruct(s, t) if i in free else pltpu.HBM(s, t) for i, (s, t) in enumerate(outs)],
        in_specs=[SMEM] + [ANY] * len(inputs),
        out_specs=[VMEM] * len(outs),
        scratch_shapes=near + list(scratch) + [pltpu.SemaphoreType.DMA((len(inputs),))],
        compiler_params=pltpu.CompilerParams(vmem_limit_bytes=limit * 2**20),
        cost_estimate=cost,
        name=name,
    )(args[0], *inputs)


def dot(a, b, ca, cb):
    return lax.dot_general(a, b, (((ca,), (cb,)), ((), ())), precision=EXACT, preferred_element_type=f32)


def thirds(x):
    hi = x.astype(bf16).astype(f32)
    mid = (x - hi).astype(bf16).astype(f32)
    return hi, mid, x - hi - mid


def pack_kernel(ids, q_ref, do_ref, o_ref, kv_ref, rq_ref, rk_ref, rv_ref, a_ref, *outs):
    *outs, mine, tables = outs
    row = lax.broadcasted_iota(jnp.int32, (EXTRA, HD), 0)
    ones = jnp.ones((EXTRA, HD), f32)

    def rows_of(x):
        hi, mid, lo = thirds(x)
        return jnp.where(row == 0, hi, jnp.where(row == 1, mid, jnp.where(row == 2, lo, 0.0))).astype(bf16)

    for k, out in enumerate(outs):

        @pl.when(pl.program_id(0) == k)
        def _():
            out[0:TOK, 0:WIDE] = q_ref[...]
            out[0:TOK, WIDE : 2 * WIDE] = do_ref[...]
            for h in range(GROUP):
                cols = slice(h * HD, (h + 1) * HD)
                product = do_ref[:, cols].astype(f32) * o_ref[:, cols].astype(f32)
                out[TOK : TOK + EXTRA, cols] = rows_of(dot(ones, product, 1, 1))
            out[TOK : TOK + EXTRA, WIDE : 2 * WIDE] = jnp.zeros((EXTRA, WIDE), bf16)

    @pl.when(pl.program_id(0) == 0)
    def _():
        head = ids[0]
        q = rq_ref[...].astype(f32) * SCALE
        k = rk_ref[...].astype(f32)
        v = rv_ref[...].astype(f32)
        pick = lax.broadcasted_iota(jnp.int32, a_ref.shape, 0) == head
        a = jnp.sum(jnp.where(pick, a_ref[...], 0.0), axis=0, keepdims=True)
        a = jnp.broadcast_to(a, (HD, TOK))
        t = lax.broadcasted_iota(jnp.int32, (TOK, TOK), 0)
        s = lax.broadcasted_iota(jnp.int32, (TOK, TOK), 1)
        cum = dot((s <= t).astype(f32), a, 1, 1)
        across = dot(a, (t <= s).astype(f32), 1, 0)
        decay = jnp.exp(jnp.where(s <= t, cum - across, -jnp.inf))
        total = cum[TOK - 1 : TOK, :]
        state = dot(k * jnp.exp(total - cum), v, 0, 0)
        tables[0] = q
        tables[1] = k
        tables[2] = cum
        tables[3] = decay
        tables[4] = decay * dot(q, k, 1, 1)
        tables[5] = state
        total = rows_of(jnp.broadcast_to(total, (EXTRA, HD)))
        mine[0:TOK, :] = kv_ref[...]
        high = state.astype(bf16)
        mine[TOK : TOK + HD, :] = high
        mine[TOK + HD : TOK + 2 * HD, :] = (state - high.astype(f32)).astype(bf16)
        mine[TOK + 2 * HD :, :] = total


def pack_rows(ids, queries, grad_out, attn_out, shared_kv, ret_query, ret_key, ret_value, log_decay):
    pack = (TOK + EXTRA, 2 * WIDE)
    mine = (TOK + 2 * HD + EXTRA, HD)
    tables = (6, TOK, HD)
    rows = pl.BlockSpec((TOK, WIDE), lambda k, ids: (0, lax.rem(ids[0] + k, 4)))
    own = pl.BlockSpec((TOK, HD), lambda k, ids: (0, ids[0]))
    whole = lambda shape: pl.BlockSpec(shape, lambda k, ids: (0,) * len(shape))
    args = (queries, grad_out, attn_out, shared_kv, ret_query, ret_key, ret_value, log_decay)
    return pl.pallas_call(
        pack_kernel,
        out_shape=[pltpu.HBM(pack, bf16)] * 4 + [pltpu.HBM(mine, bf16), pltpu.HBM(tables, f32)],
        grid_spec=pltpu.PrefetchScalarGridSpec(
            num_scalar_prefetch=1,
            grid=(4,),
            in_specs=[rows] * 3 + [whole(shared_kv.shape), own, own, whole(ret_value.shape), whole(log_decay.shape)],
            out_specs=[whole(pack)] * 4 + [whole(mine), whole(tables)],
        ),
        compiler_params=pltpu.CompilerParams(vmem_limit_bytes=16 * 2**20),
        name="pack_rows",
    )(ids, *map(in_hbm, args))


def copies_kernel(ids, theirs_ref, mine_ref, out_ref):
    for i in range(out_ref.shape[0]):
        out_ref[i, 0] = mine_ref[...]
        out_ref[i, 1] = theirs_ref[...]


def place_of(ids, b):
    low = lax.rem(lax.div(b, 4), 2)
    return lax.div(b, 8) * 4 + lax.rem(b, 4), lax.rem(low + lax.div(ids[1], 4), 2)


def attn_kernel(count, B, T, *refs):
    ids, own, other = refs[:3]
    packs, dqs = refs[3 : 3 + count], refs[3 + count : 3 + 2 * count]
    keep, send, ks, vs, kt, qs, dos, delta, p_s, dq_s, dk, dv = refs[3 + 2 * count :]
    c, core = ids[1], ids[2]

    def fill(out, ref):
        def one(b, _):
            i, p = place_of(ids, b)
            out[pl.ds(pl.multiple_of(b * TOK, TOK), TOK), :] = ref[i, p]
            return 0

        lax.fori_loop(0, BLOCKS, one, 0)

    @pl.when(core == 0)
    def _():
        fill(ks, own)
        fill(vs, other)

    @pl.when(core != 0)
    def _():
        fill(ks, other)
        fill(vs, own)

    for r in range(0, ks.shape[0], 512):
        kt[:, r : r + 512] = ks[r : r + 512, :].T
    for i in range(count):
        for h in range(GROUP):
            r = (i * GROUP + h) * TOK
            qs[r : r + TOK, :] = packs[i][0:TOK, h * HD : (h + 1) * HD]
            dos[r : r + TOK, :] = packs[i][0:TOK, (GROUP + h) * HD : (GROUP + h + 1) * HD]
        d = packs[i][TOK : TOK + EXTRA, 0:WIDE].astype(f32)
        delta[0:1, i * WIDE : (i + 1) * WIDE] = d[0:1] + d[1:2] + d[2:3]
    dk[...] = jnp.zeros_like(dk)
    dv[...] = jnp.zeros_like(dv)
    blocks = (c * TOK + TOK + B - 1) // B

    def tile(t, _):
        t0 = pl.multiple_of(t * T, T)
        q = qs[pl.ds(t0, T), :]
        do = dos[pl.ds(t0, T), :]
        dl = delta[0:1, pl.ds(t0, T)]

        def scores(j, m, masked):
            j0 = pl.multiple_of(j * B, B)
            s = lax.dot_general(ks[pl.ds(j0, B), :], q, (((1,), (1,)), ((), ())), preferred_element_type=f32)
            s = s * (SCALE * LOG2E)
            if masked:
                key = j0 + lax.broadcasted_iota(jnp.int32, (B, T), 0)
                row = c * TOK + (lax.broadcasted_iota(jnp.int32, (B, T), 1) & (TOK - 1))
                s = jnp.where(key <= row, s, -jnp.inf)
            p_s[pl.ds(j0, B), :] = s
            return jnp.maximum(m, jnp.max(s, axis=0, keepdims=True))

        m = jnp.full((1, T), -jnp.inf, f32)
        m = lax.fori_loop(0, blocks - 1, lambda j, m: scores(j, m, False), m)
        m = scores(blocks - 1, m, True)

        def exponents(j, total):
            rows = pl.ds(pl.multiple_of(j * B, B), B)
            e = jnp.exp2(p_s[rows, :] - m)
            p_s[rows, :] = e
            return total + jnp.sum(e, axis=0, keepdims=True)

        inverse = 1.0 / lax.fori_loop(0, blocks, exponents, jnp.zeros((1, T), f32))
        dq_s[...] = jnp.zeros_like(dq_s)

        def backward(j, _):
            j0 = pl.multiple_of(j * B, B)
            rows = pl.ds(j0, B)
            w = p_s[rows, :] * inverse
            dp = lax.dot_general(vs[rows, :], do, (((1,), (1,)), ((), ())), preferred_element_type=f32)
            ds = (w * (dp - dl)).astype(bf16)
            dv[rows, :] += jnp.dot(w.astype(bf16), do, preferred_element_type=f32).astype(bf16).astype(f32)
            part = jnp.dot(ds, q, preferred_element_type=f32) * SCALE
            dk[rows, :] += part.astype(bf16).astype(f32)
            dq_s[...] += jnp.dot(kt[:, rows], ds, preferred_element_type=f32)
            return 0

        lax.fori_loop(0, blocks, backward, 0)
        for r in range(0, T, TOK):
            qs[pl.ds(t0 + r, TOK), :] = (dq_s[:, r : r + TOK].T * SCALE).astype(bf16)
        return 0

    lax.fori_loop(0, count * WIDE // T, tile, 0)
    for i in range(count):
        for h in range(GROUP):
            r = (i * GROUP + h) * TOK
            dqs[i][:, h * HD : (h + 1) * HD] = qs[r : r + TOK, :]

    @pl.when(core == 0)
    def _():
        keep[...] = dk[...]
        send[...] = dv[...]

    @pl.when(core != 0)
    def _():
        keep[...] = dv[...]
        send[...] = dk[...]


def attention(ids, own, other, packs, B=1024, T=WIDE):
    count, length, rows = len(packs), BLOCKS * TOK, len(packs) * WIDE
    got = call(
        functools.partial(attn_kernel, count, B, T),
        [((TOK, WIDE), bf16)] * count + [((length, HD), f32)] * 2,
        [ids, own, other, *packs],
        "attention",
        1 + count,
        [
            pltpu.VMEM((length, HD), bf16),
            pltpu.VMEM((length, HD), bf16),
            pltpu.VMEM((HD, length), bf16),
            pltpu.VMEM((rows, HD), bf16),
            pltpu.VMEM((rows, HD), bf16),
            pltpu.VMEM((8, rows), f32),
            pltpu.VMEM((length, T), f32),
            pltpu.VMEM((HD, T), f32),
            pltpu.VMEM((length, HD), f32),
            pltpu.VMEM((length, HD), f32),
        ],
        limit=50,
        flops=10 * rows * length * HD,
        nbytes=12 * length * HD,
        free=(count, count + 1),
    )
    return got[:count], got[count:]


def retain_kernel(ids, all_ref, tables, v_ref, out_ref, totals_ref):
    def step(b, state):
        i, p = place_of(ids, b)
        added = all_ref[i, p, TOK : TOK + 2 * HD, :].astype(f32)
        return jnp.exp(totals_ref[pl.ds(b, 1), :]) * state + (added[0:HD] + added[HD:])

    for b in range(BLOCKS):
        i, p = place_of(ids, jnp.int32(b))
        totals_ref[b : b + 1, :] = jnp.sum(all_ref[i, p, TOK + 2 * HD :, :].astype(f32), axis=0, keepdims=True)
    state = lax.fori_loop(0, ids[1], step, jnp.zeros((HD, HD), f32))
    q, cum, inner = tables[0], tables[2], tables[4]
    out_ref[0] = state
    out_ref[1] = jnp.exp(cum[TOK - 1 : TOK, :]) * state + tables[5]
    out_ref[2] = dot(inner, v_ref[...].astype(f32), 1, 0) + dot(q * jnp.exp(cum), state, 1, 0)


def norm_kernel(ids, parts_ref, states, tables, out_ref, carry_ref):
    def add(i, total):
        return total + parts_ref[i].astype(f32)

    upstream = lax.fori_loop(1, BLOCKS, add, parts_ref[0].astype(f32))
    retained = states[2]
    inverse = lax.rsqrt(jnp.mean(retained * retained, axis=1, keepdims=True) + 1e-06)
    normed = retained * inverse
    grad = (upstream - normed * jnp.mean(normed * upstream, axis=1, keepdims=True)) * inverse
    out_ref[...] = grad
    carry_ref[...] = dot(tables[0] * jnp.exp(tables[2]), grad, 0, 0)


def decay_over(totals, low, high):
    add = lambda m, total: total + totals[pl.ds(m, 1), :]
    return jnp.exp(lax.fori_loop(low, high, add, jnp.zeros((1, HD), f32)))


def scan_x_kernel(ids, r1, r2, r3, carry_ref, totals, group_ref, out_ref, held):
    c = ids[1]
    x = lax.rem(c, 4)
    for k, ref in enumerate((carry_ref, r1, r2, r3)):
        held[k] = ref[...]

    def step(i, grad):
        m = 3 - i
        return held[lax.rem(m - x + 4, 4)] + jnp.exp(totals[pl.ds(c - x + m, 1), :]) * grad

    zero = jnp.zeros((HD, HD), f32)
    group_ref[...] = lax.fori_loop(0, 4, step, zero)
    out_ref[...] = lax.fori_loop(0, 3 - x, step, zero)


def scan_z_kernel(ids, theirs_ref, mine_ref, leaving_ref, totals, both_ref, out_ref):
    c = ids[1]
    first = lax.rem(lax.div(c, 4), 2) == 0
    start = lax.div(c, 8) * 8
    theirs, mine = theirs_ref[...], mine_ref[...]
    low, high = jnp.where(first, mine, theirs), jnp.where(first, theirs, mine)
    both_ref[...] = low + decay_over(totals, start, start + 4) * high
    out_ref[...] = leaving_ref[...] + jnp.where(first, decay_over(totals, c + 1, start + 4) * theirs, 0.0)


def grads_kernel(
    ids, r1, r2, r3, leaving_ref, totals, grad_ref, states, tables, v_ref, dv_ref, part_ref, held
):
    c = ids[1]
    y = lax.div(c, 8)
    for k, ref in enumerate((r1, r2, r3)):
        held[k] = ref[...]

    def step(i, later):
        m = 3 - i
        return held[m - y - 1] + decay_over(totals, m * 8, m * 8 + 8) * later

    later = lax.fori_loop(0, 3 - y, step, jnp.zeros((HD, HD), f32))
    leaving = leaving_ref[...] + decay_over(totals, c + 1, y * 8 + 8) * later
    grad, state = grad_ref[...], states[0]
    q, k, cum, decay, inner = (tables[i] for i in range(5))
    v = v_ref[...].astype(f32)
    total = cum[TOK - 1 : TOK, :]
    tail = jnp.exp(total - cum)
    pair = decay * dot(grad, v, 1, 1)
    dq = jnp.exp(cum) * dot(grad, state, 1, 1) + dot(pair, k, 1, 0)
    dk = dot(pair, q, 0, 0) + tail * dot(v, leaving, 1, 1)
    dv_ref[...] = dot(inner, grad, 0, 0) + tail * dot(k, leaving, 1, 0)
    through = jnp.sum(jnp.sum(leaving * states[1], axis=1, keepdims=True), axis=0, keepdims=True)
    change = jnp.sum(grad * states[2], axis=1, keepdims=True) - jnp.sum(k * dk, axis=1, keepdims=True)
    t = lax.broadcasted_iota(jnp.int32, (TOK, TOK), 0)
    s = lax.broadcasted_iota(jnp.int32, (TOK, TOK), 1)
    da = dot(jnp.broadcast_to(change, (TOK, HD)), (s <= t).astype(f32), 0, 0) + through
    part_ref[0:TOK, 0:HD] = dq * SCALE
    part_ref[0:TOK, HD : 2 * HD] = dk
    part_ref[TOK : TOK + EXTRA, 0:HD] = da[0:EXTRA]
    part_ref[TOK : TOK + EXTRA, HD : 2 * HD] = jnp.zeros((EXTRA, HD), f32)


def message_kernel(ids, a_ref, b_ref, out_ref):
    out_ref[0:TOK, :] = (a_ref[0:TOK, :] + b_ref[0:TOK, :]).astype(bf16)
    tail = slice(TOK, TOK + EXTRA)
    hi, mid, lo = thirds(a_ref[tail, :] + b_ref[tail, :])
    row = lax.broadcasted_iota(jnp.int32, hi.shape, 0)
    parts = jnp.where(row == 0, hi, jnp.where(row == 1, mid, jnp.where(row == 2, lo, 0.0)))
    out_ref[tail, :] = parts.astype(bf16)


def finish_kernel(ids, *refs):
    messages, (dq_ref, dk_ref, da_ref) = refs[:4], refs[4:]
    row = lax.broadcasted_iota(jnp.int32, da_ref.shape, 0)
    da = jnp.zeros(da_ref.shape, f32)
    for k, ref in enumerate(messages):
        head = lax.rem(ids[0] + 3 - k, 4)
        cols = pl.ds(pl.multiple_of(head * HD, HD), HD)
        dq_ref[:, cols] = ref[0:TOK, 0:HD].astype(f32)
        dk_ref[:, cols] = ref[0:TOK, HD : 2 * HD].astype(f32)
        value = jnp.sum(ref[TOK : TOK + EXTRA, 0:HD].astype(f32), axis=0, keepdims=True)
        da = jnp.where(row == head, value, da)
    da_ref[...] = da


def rows_kernel(ids, *refs):
    parts, out = refs[:4], refs[4]
    for k, ref in enumerate(parts):
        start = pl.multiple_of(lax.rem(ids[0] + 1 + k, 4) * WIDE, HD)
        out[:, pl.ds(start, WIDE)] = ref[...]


def shift(x, k):
    return lax.ppermute(x, "zhi", [(i, (i + k) % 4) for i in range(4)])


def from_next(x, axis, k):
    return lax.ppermute(x, axis, [(i, (i - k) % 4) for i in range(4)])


def swap(x):
    return lax.ppermute(x, "core", [(0, 1), (1, 0)])


def spread(x):
    return lax.all_to_all(x, CTX, 0, 0)


def on_device(queries, attn_out, grad_out, shared_kv, ret_query, ret_key, ret_value, log_decay):
    z = lax.axis_index("zhi")
    ids = jnp.stack([z, lax.axis_index(CTX), lax.axis_index("core")]).astype(jnp.int32)
    *packs, mine, tables = pack_rows(
        ids, queries[0], grad_out[0], attn_out[0], shared_kv, ret_query, ret_key, ret_value, log_decay.T
    )
    from1, from3, from2 = shift(packs[1], 1), shift(packs[3], 3), shift(packs[2], 2)
    theirs = lax.ppermute(mine, "zlo", [(0, 1), (1, 0)])
    (copies,) = call(copies_kernel, [((16, 2, *mine.shape), bf16)], [ids, theirs, mine], "copies", 1)
    blocks = lax.all_to_all(copies, ("y", "x"), 0, 0)
    own = blocks[:, :, 0:TOK]
    own, from1, from3, from2 = lax.optimization_barrier((own, from1, from3, from2))
    other = swap(own)
    (dq1, dq3, dq2, dq0), (keep, send) = attention(ids, own, other, [from1, from3, from2, packs[0]])
    back1, back3, back2 = shift(dq1, 3), shift(dq3, 1), shift(dq2, 2)

    square = ((TOK, HD), f32)
    states, totals = call(
        retain_kernel, [((3, TOK, HD), f32), ((BLOCKS, HD), f32)], [ids, blocks, tables, ret_value], "retention_forward", 1
    )
    part = (keep + swap(send)).astype(bf16)
    parts = spread(part.reshape(BLOCKS, TOK, HD))
    parts, back1, back3 = lax.optimization_barrier((parts, back1, back3))
    grad, carry = call(
        norm_kernel, [square] * 2, [ids, parts, states, tables], "norm_backward", 1, free=(1,)
    )
    held = pltpu.VMEM((4, HD, HD), f32)
    near = [from_next(carry, "x", k) for k in (1, 2, 3)]
    group, leaving = call(scan_x_kernel, [square] * 2, [ids, *near, carry, totals], "scan_x", 4, [held], free=(0, 1))
    theirs = lax.ppermute(group, "zlo", [(0, 1), (1, 0)])
    both, leaving = call(scan_z_kernel, [square] * 2, [ids, theirs, group, leaving, totals], "scan_z", 3, free=(0, 1))
    far = [from_next(both, "y", k) for k in (1, 2, 3)]
    *far, back2 = lax.optimization_barrier((*far, back2))
    d_value, half = call(
        grads_kernel,
        [square, ((TOK + EXTRA, 2 * HD), f32)],
        [ids, *far, leaving, totals, grad, states, tables, ret_value],
        "retention_grads",
        4,
        [held],
        free=(1,),
    )
    (message,) = call(
        message_kernel, [((TOK + EXTRA, 2 * HD), bf16)], [ids, swap(half), half], "message", 2, free=(0,)
    )
    d_query, d_key, d_decay = call(
        finish_kernel,
        [(ret_query.shape, f32), (ret_key.shape, f32), (log_decay.shape[::-1], f32)],
        [ids, *(shift(message, k) for k in (1, 2, 3)), message],
        "finish",
        4,
    )
    (d_queries,) = call(
        rows_kernel, [((TOK, 4 * WIDE), bf16)], [ids, back1, back2, back3, dq0], "query_rows", 3
    )
    return d_queries[None], d_query, d_key, d_value, d_decay.T


def solution(mesh):
    fine = Mesh(mesh.devices.reshape(4, 2, 4, 2, 4), ("zhi", "core", "y", "zlo", "x"))
    section = ("zhi", "core")
    rows = P(section, CTX, None)
    return jax.shard_map(
        on_device,
        mesh=fine,
        in_specs=(rows, rows, rows, P(CTX, section), P(CTX, None), P(CTX, None), P(CTX, section), P(CTX, None)),
        out_specs=(rows, P(CTX, None), P(CTX, None), P(CTX, section), P(CTX, None)),
        check_vma=False,
    )
```

```python
import functools
import math

import jax
import jax.numpy as jnp
from jax import lax
from jax.experimental import pallas as pl
from jax.experimental.pallas import tpu as pltpu
from jax.sharding import Mesh, PartitionSpec as P

bf16 = jnp.bfloat16
f32 = jnp.float32
EXACT = lax.Precision.HIGHEST
TOK = 128
HD = 128
GROUP = 5
WIDE = GROUP * HD
EXTRA = 16
BLOCKS = 32
SCALE = HD**-0.5
LOG2E = math.log2(math.e)
CTX = ("y", "zlo", "x")
VMEM = pl.BlockSpec(memory_space=pltpu.VMEM)
SMEM = pl.BlockSpec(memory_space=pltpu.SMEM)


ANY = pl.BlockSpec(memory_space=pl.ANY)


def in_hbm(x):
    return pltpu.with_memory_space_constraint(x, pltpu.HBM)


def loaded(kernel, inputs, outputs, *refs):
    ids, far, rest = refs[0], refs[1 : 1 + inputs], refs[1 + inputs :]
    results, near, scratch = rest[:outputs], rest[outputs : outputs + inputs], rest[outputs + inputs : -1]
    copies = [pltpu.make_async_copy(f, n, rest[-1].at[i]) for i, (f, n) in enumerate(zip(far, near))]
    for copy in copies:
        copy.start()
    for copy in copies:
        copy.wait()
    kernel(ids, *near, *results, *scratch)


def call(kernel, outs, args, name, loose=0, scratch=(), limit=8, flops=0, nbytes=0, free=()):
    cost = None
    if flops:
        cost = pl.CostEstimate(flops=flops, bytes_accessed=nbytes, transcendentals=0)
    inputs = [x if i < loose else in_hbm(x) for i, x in enumerate(args[1:])]
    near = [pltpu.VMEM(x.shape, x.dtype) for x in inputs]
    return pl.pallas_call(
        functools.partial(loaded, kernel, len(inputs), len(outs)),
        out_shape=[jax.ShapeDtypeStruct(s, t) if i in free else pltpu.HBM(s, t) for i, (s, t) in enumerate(outs)],
        in_specs=[SMEM] + [ANY] * len(inputs),
        out_specs=[VMEM] * len(outs),
        scratch_shapes=near + list(scratch) + [pltpu.SemaphoreType.DMA((len(inputs),))],
        compiler_params=pltpu.CompilerParams(vmem_limit_bytes=limit * 2**20),
        cost_estimate=cost,
        name=name,
    )(args[0], *inputs)


def dot(a, b, ca, cb):
    return lax.dot_general(a, b, (((ca,), (cb,)), ((), ())), precision=EXACT, preferred_element_type=f32)


def thirds(x):
    hi = x.astype(bf16).astype(f32)
    mid = (x - hi).astype(bf16).astype(f32)
    return hi, mid, x - hi - mid


def rows_of(x):
    row = lax.broadcasted_iota(jnp.int32, x.shape, 0)
    hi, mid, lo = thirds(x)
    return jnp.where(row == 0, hi, jnp.where(row == 1, mid, jnp.where(row == 2, lo, 0.0))).astype(bf16)


def local_kernel(ids, kv_ref, rq_ref, rk_ref, rv_ref, a_ref, mine, tables):
    head = ids[0]
    cols = pl.ds(pl.multiple_of(head * HD, HD), HD)
    q = rq_ref[:, cols].astype(f32) * SCALE
    k = rk_ref[:, cols].astype(f32)
    v = rv_ref[...].astype(f32)
    pick = lax.broadcasted_iota(jnp.int32, a_ref.shape, 0) == head
    a = jnp.sum(jnp.where(pick, a_ref[...], 0.0), axis=0, keepdims=True)
    a = jnp.broadcast_to(a, (HD, TOK))
    t = lax.broadcasted_iota(jnp.int32, (TOK, TOK), 0)
    s = lax.broadcasted_iota(jnp.int32, (TOK, TOK), 1)
    cum = dot((s <= t).astype(f32), a, 1, 1)
    across = dot(a, (t <= s).astype(f32), 1, 0)
    decay = jnp.exp(jnp.where(s <= t, cum - across, -jnp.inf))
    total = cum[TOK - 1 : TOK, :]
    state = dot(k * jnp.exp(total - cum), v, 0, 0)
    mine[0:TOK, :] = kv_ref[...]
    mine[TOK : TOK + HD, :] = state.astype(bf16)
    mine[TOK + HD :, :] = rows_of(jnp.broadcast_to(total, (EXTRA, HD)))
    tables[0] = q
    tables[1] = k
    tables[2] = cum
    tables[3] = decay
    tables[4] = decay * dot(q, k, 1, 1)
    tables[5] = state


def pack_kernel(ids, q_ref, do_ref, o_ref, *outs):
    ones = jnp.ones((EXTRA, HD), bf16)
    for k, out in enumerate(outs):

        @pl.when(pl.program_id(0) == k)
        def _():
            out[0:TOK, 0:WIDE] = q_ref[...]
            out[0:TOK, WIDE : 2 * WIDE] = do_ref[...]
            for h in range(GROUP):
                cols = slice(h * HD, (h + 1) * HD)
                product = do_ref[:, cols].astype(f32) * o_ref[:, cols].astype(f32)
                hi = product.astype(bf16)
                lo = (product - hi.astype(f32)).astype(bf16)
                delta = [
                    lax.dot_general(ones, x, (((1,), (1,)), ((), ())), preferred_element_type=f32) for x in (hi, lo)
                ]
                out[TOK : TOK + EXTRA, cols] = rows_of(delta[0] + delta[1])
            out[TOK : TOK + EXTRA, WIDE : 2 * WIDE] = jnp.zeros((EXTRA, WIDE), bf16)


def pack_rows(ids, *args):
    pack = (TOK + EXTRA, 2 * WIDE)
    rows = pl.BlockSpec((TOK, WIDE), lambda k, ids: (0, lax.rem(ids[0] + k, 4)))
    return pl.pallas_call(
        pack_kernel,
        out_shape=[pltpu.HBM(pack, bf16)] * 4,
        grid_spec=pltpu.PrefetchScalarGridSpec(
            num_scalar_prefetch=1,
            grid=(4,),
            in_specs=[rows] * 3,
            out_specs=[pl.BlockSpec(pack, lambda k, ids: (0, 0))] * 4,
        ),
        compiler_params=pltpu.CompilerParams(vmem_limit_bytes=16 * 2**20),
        name="pack_rows",
    )(ids, *map(in_hbm, args))


def copies_kernel(ids, theirs_ref, mine_ref, out_ref):
    for i in range(out_ref.shape[0]):
        out_ref[i, 0] = mine_ref[...]
        out_ref[i, 1] = theirs_ref[...]


def place_of(ids, b):
    low = lax.rem(lax.div(b, 4), 2)
    return lax.div(b, 8) * 4 + lax.rem(b, 4), lax.rem(low + lax.div(ids[1], 4), 2)


def attn_kernel(count, B, T, *refs):
    ids, own, other = refs[:3]
    packs, dqs = refs[3 : 3 + count], refs[3 + count : 3 + 2 * count]
    keep, send, ks, vs, kt, qs, dos, delta, p_s, dq_s, dk, dv = refs[3 + 2 * count :]
    c, core = ids[1], ids[2]

    def fill(out, ref):
        def one(b, _):
            i, p = place_of(ids, b)
            out[pl.ds(pl.multiple_of(b * TOK, TOK), TOK), :] = ref[i, p]
            return 0

        lax.fori_loop(0, BLOCKS, one, 0)

    @pl.when(core == 0)
    def _():
        fill(ks, own)
        fill(vs, other)

    @pl.when(core != 0)
    def _():
        fill(ks, other)
        fill(vs, own)

    for r in range(0, ks.shape[0], 512):
        kt[:, r : r + 512] = ks[r : r + 512, :].T
    for i in range(count):
        for h in range(GROUP):
            r = (i * GROUP + h) * TOK
            qs[r : r + TOK, :] = packs[i][0:TOK, h * HD : (h + 1) * HD]
            dos[r : r + TOK, :] = packs[i][0:TOK, (GROUP + h) * HD : (GROUP + h + 1) * HD]
        d = packs[i][TOK : TOK + EXTRA, 0:WIDE].astype(f32)
        delta[0:1, i * WIDE : (i + 1) * WIDE] = d[0:1] + d[1:2] + d[2:3]
    dk[...] = jnp.zeros_like(dk)
    dv[...] = jnp.zeros_like(dv)
    turned = c + 8 * (3 - 2 * lax.div(c, 8))

    def tile(t, _):
        at = jnp.where(t < count // 2, turned, c)
        blocks = lax.div(at * TOK + TOK + B - 1, B)
        t0 = pl.multiple_of(t * T, T)
        q = qs[pl.ds(t0, T), :]
        do = dos[pl.ds(t0, T), :]
        dl = delta[0:1, pl.ds(t0, T)]

        def scores(j, m, masked):
            j0 = pl.multiple_of(j * B, B)
            s = lax.dot_general(ks[pl.ds(j0, B), :], q, (((1,), (1,)), ((), ())), preferred_element_type=f32)
            s = s * (SCALE * LOG2E)
            if masked:
                key = j0 + lax.broadcasted_iota(jnp.int32, (B, T), 0)
                row = at * TOK + (lax.broadcasted_iota(jnp.int32, (B, T), 1) & (TOK - 1))
                s = jnp.where(key <= row, s, -jnp.inf)
            p_s[pl.ds(j0, B), :] = s
            return jnp.maximum(m, jnp.max(s, axis=0, keepdims=True))

        m = jnp.full((1, T), -jnp.inf, f32)
        m = lax.fori_loop(0, blocks - 1, lambda j, m: scores(j, m, False), m)
        m = scores(blocks - 1, m, True)

        def exponents(j, total):
            rows = pl.ds(pl.multiple_of(j * B, B), B)
            e = jnp.exp2(p_s[rows, :] - m)
            p_s[rows, :] = e
            return total + jnp.sum(e, axis=0, keepdims=True)

        inverse = 1.0 / lax.fori_loop(0, blocks, exponents, jnp.zeros((1, T), f32))
        dq_s[...] = jnp.zeros_like(dq_s)

        def backward(j, _):
            j0 = pl.multiple_of(j * B, B)
            rows = pl.ds(j0, B)
            w = p_s[rows, :] * inverse
            dp = lax.dot_general(vs[rows, :], do, (((1,), (1,)), ((), ())), preferred_element_type=f32)
            ds = (w * (dp - dl)).astype(bf16)
            dv[rows, :] += jnp.dot(w.astype(bf16), do, preferred_element_type=f32).astype(bf16).astype(f32)
            part = jnp.dot(ds, q, preferred_element_type=f32) * SCALE
            dk[rows, :] += part.astype(bf16).astype(f32)
            dq_s[...] += jnp.dot(kt[:, rows], ds, preferred_element_type=f32)
            return 0

        lax.fori_loop(0, blocks, backward, 0)
        for r in range(0, T, TOK):
            qs[pl.ds(t0 + r, TOK), :] = (dq_s[:, r : r + TOK].T * SCALE).astype(bf16)
        return 0

    lax.fori_loop(0, count * WIDE // T, tile, 0)
    for i in range(count):
        for h in range(GROUP):
            r = (i * GROUP + h) * TOK
            dqs[i][:, h * HD : (h + 1) * HD] = qs[r : r + TOK, :]

    @pl.when(core == 0)
    def _():
        keep[...] = dk[...]
        send[...] = dv[...].astype(bf16)

    @pl.when(core != 0)
    def _():
        keep[...] = dv[...]
        send[...] = dk[...].astype(bf16)


def attention(ids, own, other, packs, B=1024, T=WIDE):
    count, length, rows = len(packs), BLOCKS * TOK, len(packs) * WIDE
    got = call(
        functools.partial(attn_kernel, count, B, T),
        [((TOK, WIDE), bf16)] * count + [((length, HD), f32), ((length, HD), bf16)],
        [ids, own, other, *packs],
        "attention",
        1 + count,
        [
            pltpu.VMEM((length, HD), bf16),
            pltpu.VMEM((length, HD), bf16),
            pltpu.VMEM((HD, length), bf16),
            pltpu.VMEM((rows, HD), bf16),
            pltpu.VMEM((rows, HD), bf16),
            pltpu.VMEM((8, rows), f32),
            pltpu.VMEM((length, T), f32),
            pltpu.VMEM((HD, T), f32),
            pltpu.VMEM((length, HD), f32),
            pltpu.VMEM((length, HD), f32),
        ],
        limit=44,
        flops=10 * rows * length * HD,
        nbytes=12 * length * HD,
        free=(count, count + 1),
    )
    return got[:count], got[count:]


def retain_kernel(ids, all_ref, tables, v_ref, out_ref, totals_ref):
    def step(b, state):
        i, p = place_of(ids, b)
        return jnp.exp(totals_ref[pl.ds(b, 1), :]) * state + all_ref[i, p, TOK : TOK + HD, :].astype(f32)

    for b in range(BLOCKS):
        i, p = place_of(ids, jnp.int32(b))
        totals_ref[b : b + 1, :] = jnp.sum(all_ref[i, p, TOK + HD :, :].astype(f32), axis=0, keepdims=True)
    state = lax.fori_loop(0, ids[1], step, jnp.zeros((HD, HD), f32))
    q, cum, inner = tables[0], tables[2], tables[4]
    out_ref[0] = state
    out_ref[1] = jnp.exp(cum[TOK - 1 : TOK, :]) * state + tables[5]
    out_ref[2] = dot(inner, v_ref[...].astype(f32), 1, 0) + dot(q * jnp.exp(cum), state, 1, 0)


def norm_kernel(ids, parts_ref, states, tables, out_ref, carry_ref):
    def add(i, total):
        return total + parts_ref[i].astype(f32)

    upstream = lax.fori_loop(1, BLOCKS, add, parts_ref[0].astype(f32))
    retained = states[2]
    inverse = lax.rsqrt(jnp.mean(retained * retained, axis=1, keepdims=True) + 1e-06)
    normed = retained * inverse
    grad = (upstream - normed * jnp.mean(normed * upstream, axis=1, keepdims=True)) * inverse
    out_ref[...] = grad
    carry_ref[...] = dot(tables[0] * jnp.exp(tables[2]), grad, 0, 0)


def decay_over(totals, low, high):
    add = lambda m, total: total + totals[pl.ds(m, 1), :]
    return jnp.exp(lax.fori_loop(low, high, add, jnp.zeros((1, HD), f32)))


def scan_x_kernel(ids, r1, r2, r3, carry_ref, totals, group_ref, out_ref, held):
    c = ids[1]
    x = lax.rem(c, 4)
    for k, ref in enumerate((carry_ref, r1, r2, r3)):
        held[k] = ref[...]

    def step(i, grad):
        m = 3 - i
        return held[lax.rem(m - x + 4, 4)] + jnp.exp(totals[pl.ds(c - x + m, 1), :]) * grad

    zero = jnp.zeros((HD, HD), f32)
    group_ref[...] = lax.fori_loop(0, 4, step, zero)
    out_ref[...] = lax.fori_loop(0, 3 - x, step, zero)


def scan_z_kernel(ids, theirs_ref, mine_ref, leaving_ref, totals, both_ref, out_ref):
    c = ids[1]
    first = lax.rem(lax.div(c, 4), 2) == 0
    start = lax.div(c, 8) * 8
    theirs, mine = theirs_ref[...], mine_ref[...]
    low, high = jnp.where(first, mine, theirs), jnp.where(first, theirs, mine)
    both_ref[...] = low + decay_over(totals, start, start + 4) * high
    out_ref[...] = leaving_ref[...] + jnp.where(first, decay_over(totals, c + 1, start + 4) * theirs, 0.0)


def grads_kernel(
    ids, r1, r2, r3, leaving_ref, totals, grad_ref, states, tables, v_ref, dv_ref, part_ref, held
):
    c = ids[1]
    y = lax.div(c, 8)
    for k, ref in enumerate((r1, r2, r3)):
        held[k] = ref[...]

    def step(i, later):
        m = 3 - i
        return held[m - y - 1] + decay_over(totals, m * 8, m * 8 + 8) * later

    later = lax.fori_loop(0, 3 - y, step, jnp.zeros((HD, HD), f32))
    leaving = leaving_ref[...] + decay_over(totals, c + 1, y * 8 + 8) * later
    grad, state = grad_ref[...], states[0]
    q, k, cum, decay, inner = (tables[i] for i in range(5))
    v = v_ref[...].astype(f32)
    total = cum[TOK - 1 : TOK, :]
    tail = jnp.exp(total - cum)
    pair = decay * dot(grad, v, 1, 1)
    dq = jnp.exp(cum) * dot(grad, state, 1, 1) + dot(pair, k, 1, 0)
    dk = dot(pair, q, 0, 0) + tail * dot(v, leaving, 1, 1)
    dv_ref[...] = dot(inner, grad, 0, 0) + tail * dot(k, leaving, 1, 0)
    through = jnp.sum(jnp.sum(leaving * states[1], axis=1, keepdims=True), axis=0, keepdims=True)
    change = jnp.sum(grad * states[2], axis=1, keepdims=True) - jnp.sum(k * dk, axis=1, keepdims=True)
    t = lax.broadcasted_iota(jnp.int32, (TOK, TOK), 0)
    s = lax.broadcasted_iota(jnp.int32, (TOK, TOK), 1)
    da = dot(jnp.broadcast_to(change, (TOK, HD)), (s <= t).astype(f32), 0, 0) + through
    part_ref[0:TOK, 0:HD] = dq * SCALE
    part_ref[0:TOK, HD : 2 * HD] = dk
    part_ref[TOK : TOK + EXTRA, 0:HD] = da[0:EXTRA]
    part_ref[TOK : TOK + EXTRA, HD : 2 * HD] = jnp.zeros((EXTRA, HD), f32)


def message_kernel(ids, a_ref, b_ref, out_ref):
    out_ref[0:TOK, :] = (a_ref[0:TOK, :] + b_ref[0:TOK, :]).astype(bf16)
    tail = slice(TOK, TOK + EXTRA)
    hi, mid, lo = thirds(a_ref[tail, :] + b_ref[tail, :])
    row = lax.broadcasted_iota(jnp.int32, hi.shape, 0)
    parts = jnp.where(row == 0, hi, jnp.where(row == 1, mid, jnp.where(row == 2, lo, 0.0)))
    out_ref[tail, :] = parts.astype(bf16)


def finish_kernel(ids, *refs):
    messages, (dq_ref, dk_ref, da_ref) = refs[:4], refs[4:]
    row = lax.broadcasted_iota(jnp.int32, da_ref.shape, 0)
    da = jnp.zeros(da_ref.shape, f32)
    for k, ref in enumerate(messages):
        head = lax.rem(ids[0] + 3 - k, 4)
        cols = pl.ds(pl.multiple_of(head * HD, HD), HD)
        dq_ref[:, cols] = ref[0:TOK, 0:HD].astype(f32)
        dk_ref[:, cols] = ref[0:TOK, HD : 2 * HD].astype(f32)
        value = jnp.sum(ref[TOK : TOK + EXTRA, 0:HD].astype(f32), axis=0, keepdims=True)
        da = jnp.where(row == head, value, da)
    da_ref[...] = da


def rows_kernel(ids, *refs):
    parts, out = refs[:4], refs[4]
    for k, ref in enumerate(parts):
        start = pl.multiple_of(lax.rem(ids[0] + 1 + k, 4) * WIDE, HD)
        out[:, pl.ds(start, WIDE)] = ref[...]


def shift(x, k, turn=False):
    if not turn:
        return lax.ppermute(x, "zhi", [(i, (i + k) % 4) for i in range(4)])
    pairs = [(4 * i + y, (i + k) % 4 * 4 + 3 - y) for i in range(4) for y in range(4)]
    return lax.ppermute(x, ("zhi", "y"), pairs)


def from_next(x, axis, k):
    return lax.ppermute(x, axis, [(i, (i - k) % 4) for i in range(4)])


def swap(x):
    return lax.ppermute(x, "core", [(0, 1), (1, 0)])


def spread(x):
    return lax.all_to_all(x, CTX, 0, 0)


def on_device(queries, attn_out, grad_out, shared_kv, ret_query, ret_key, ret_value, log_decay):
    z = lax.axis_index("zhi")
    ids = jnp.stack([z, lax.axis_index(CTX), lax.axis_index("core")]).astype(jnp.int32)
    mine, tables = call(
        local_kernel,
        [((TOK + HD + EXTRA, HD), bf16), ((6, TOK, HD), f32)],
        [ids, shared_kv, ret_query, ret_key, ret_value, log_decay.T],
        "retention_local",
        free=(0,),
    )
    packs = pack_rows(ids, queries[0], grad_out[0], attn_out[0])
    theirs = lax.ppermute(mine, "zlo", [(0, 1), (1, 0)])
    theirs, packs = lax.optimization_barrier((theirs, packs))
    from1, from3, from2 = shift(packs[1], 1, True), shift(packs[3], 3, True), shift(packs[2], 2)
    (copies,) = call(copies_kernel, [((16, 2, *mine.shape), bf16)], [ids, theirs, mine], "copies", 2)
    blocks = lax.all_to_all(copies, ("y", "x"), 0, 0)
    own = blocks[:, :, 0:TOK]
    own, from1, from3, from2 = lax.optimization_barrier((own, from1, from3, from2))
    other = swap(own)
    (dq1, dq3, dq2, dq0), (keep, send) = attention(ids, own, other, [from1, from3, from2, packs[0]])
    back1, back3, back2 = shift(dq1, 3, True), shift(dq3, 1, True), shift(dq2, 2)

    square = ((TOK, HD), f32)
    states, totals = call(
        retain_kernel, [((3, TOK, HD), f32), ((BLOCKS, HD), f32)], [ids, blocks, tables, ret_value], "retention_forward", 1
    )
    part = (keep + swap(send).astype(f32)).astype(bf16)
    parts = spread(part.reshape(BLOCKS, TOK, HD))
    parts, back1, back3 = lax.optimization_barrier((parts, back1, back3))
    grad, carry = call(
        norm_kernel, [square] * 2, [ids, parts, states, tables], "norm_backward", 1, free=(1,)
    )
    held = pltpu.VMEM((4, HD, HD), f32)
    near = [from_next(carry, "x", k) for k in (1, 2, 3)]
    group, leaving = call(scan_x_kernel, [square] * 2, [ids, *near, carry, totals], "scan_x", 4, [held], free=(0, 1))
    theirs = lax.ppermute(group, "zlo", [(0, 1), (1, 0)])
    both, leaving = call(scan_z_kernel, [square] * 2, [ids, theirs, group, leaving, totals], "scan_z", 3, free=(0, 1))
    far = [from_next(both, "y", k) for k in (1, 2, 3)]
    *far, back2 = lax.optimization_barrier((*far, back2))
    d_value, half = call(
        grads_kernel,
        [square, ((TOK + EXTRA, 2 * HD), f32)],
        [ids, *far, leaving, totals, grad, states, tables, ret_value],
        "retention_grads",
        4,
        [held],
        free=(1,),
    )
    (message,) = call(
        message_kernel, [((TOK + EXTRA, 2 * HD), bf16)], [ids, swap(half), half], "message", 2, free=(0,)
    )
    d_query, d_key, d_decay = call(
        finish_kernel,
        [(ret_query.shape, f32), (ret_key.shape, f32), (log_decay.shape[::-1], f32)],
        [ids, *(shift(message, k) for k in (1, 2, 3)), message],
        "finish",
        4,
    )
    (d_queries,) = call(
        rows_kernel, [((TOK, 4 * WIDE), bf16)], [ids, back1, back2, back3, dq0], "query_rows", 3
    )
    return d_queries[None], d_query, d_key, d_value, d_decay.T


def solution(mesh):
    fine = Mesh(mesh.devices.reshape(4, 2, 4, 2, 4), ("zhi", "core", "y", "zlo", "x"))
    section = ("zhi", "core")
    rows = P(section, CTX, None)
    return jax.shard_map(
        on_device,
        mesh=fine,
        in_specs=(rows, rows, rows, P(CTX, section), P(CTX, None), P(CTX, None), P(CTX, section), P(CTX, None)),
        out_specs=(rows, P(CTX, None), P(CTX, None), P(CTX, section), P(CTX, None)),
        check_vma=False,
    )
```

```python
import functools
import math

import jax
import jax.numpy as jnp
from jax import lax
from jax.experimental import pallas as pl
from jax.experimental.pallas import tpu as pltpu
from jax.sharding import Mesh, PartitionSpec as P

bf16 = jnp.bfloat16
f32 = jnp.float32
EXACT = lax.Precision.HIGHEST
TOK = 128
HD = 128
GROUP = 5
WIDE = GROUP * HD
EXTRA = 16
BLOCKS = 32
SCALE = HD**-0.5
LOG2E = math.log2(math.e)
CTX = ("y", "zlo", "x")
VMEM = pl.BlockSpec(memory_space=pltpu.VMEM)
SMEM = pl.BlockSpec(memory_space=pltpu.SMEM)


ANY = pl.BlockSpec(memory_space=pl.ANY)


def in_hbm(x):
    return pltpu.with_memory_space_constraint(x, pltpu.HBM)


def loaded(kernel, inputs, outputs, *refs):
    ids, far, rest = refs[0], refs[1 : 1 + inputs], refs[1 + inputs :]
    results, near, scratch = rest[:outputs], rest[outputs : outputs + inputs], rest[outputs + inputs : -1]
    copies = [pltpu.make_async_copy(f, n, rest[-1].at[i]) for i, (f, n) in enumerate(zip(far, near))]
    for copy in copies:
        copy.start()
    for copy in copies:
        copy.wait()
    kernel(ids, *near, *results, *scratch)


def call(kernel, outs, args, name, loose=0, scratch=(), limit=8, flops=0, nbytes=0, free=()):
    cost = None
    if flops:
        cost = pl.CostEstimate(flops=flops, bytes_accessed=nbytes, transcendentals=0)
    inputs = [x if i < loose else in_hbm(x) for i, x in enumerate(args[1:])]
    near = [pltpu.VMEM(x.shape, x.dtype) for x in inputs]
    return pl.pallas_call(
        functools.partial(loaded, kernel, len(inputs), len(outs)),
        out_shape=[jax.ShapeDtypeStruct(s, t) if i in free else pltpu.HBM(s, t) for i, (s, t) in enumerate(outs)],
        in_specs=[SMEM] + [ANY] * len(inputs),
        out_specs=[VMEM] * len(outs),
        scratch_shapes=near + list(scratch) + [pltpu.SemaphoreType.DMA((len(inputs),))],
        compiler_params=pltpu.CompilerParams(vmem_limit_bytes=limit * 2**20),
        cost_estimate=cost,
        name=name,
    )(args[0], *inputs)


def dot(a, b, ca, cb):
    return lax.dot_general(a, b, (((ca,), (cb,)), ((), ())), precision=EXACT, preferred_element_type=f32)


def thirds(x):
    hi = x.astype(bf16).astype(f32)
    mid = (x - hi).astype(bf16).astype(f32)
    return hi, mid, x - hi - mid


def rows_of(x):
    row = lax.broadcasted_iota(jnp.int32, x.shape, 0)
    hi, mid, lo = thirds(x)
    return jnp.where(row == 0, hi, jnp.where(row == 1, mid, jnp.where(row == 2, lo, 0.0))).astype(bf16)


def local_kernel(ids, kv_ref, rq_ref, rk_ref, rv_ref, a_ref, mine, tables):
    head = ids[0]
    cols = pl.ds(pl.multiple_of(head * HD, HD), HD)
    q = rq_ref[:, cols].astype(f32) * SCALE
    k = rk_ref[:, cols].astype(f32)
    v = rv_ref[...].astype(f32)
    pick = lax.broadcasted_iota(jnp.int32, a_ref.shape, 0) == head
    a = jnp.sum(jnp.where(pick, a_ref[...], 0.0), axis=0, keepdims=True)
    a = jnp.broadcast_to(a, (HD, TOK))
    t = lax.broadcasted_iota(jnp.int32, (TOK, TOK), 0)
    s = lax.broadcasted_iota(jnp.int32, (TOK, TOK), 1)
    cum = dot((s <= t).astype(f32), a, 1, 1)
    across = dot(a, (t <= s).astype(f32), 1, 0)
    decay = jnp.exp(jnp.where(s <= t, cum - across, -jnp.inf))
    total = cum[TOK - 1 : TOK, :]
    state = dot(k * jnp.exp(total - cum), v, 0, 0)
    mine[0:TOK, :] = kv_ref[...]
    mine[TOK : TOK + HD, :] = state.astype(bf16)
    mine[TOK + HD :, :] = rows_of(jnp.broadcast_to(total, (EXTRA, HD)))
    tables[0] = q
    tables[1] = k
    tables[2] = cum
    tables[3] = decay
    tables[4] = decay * dot(q, k, 1, 1)
    tables[5] = state


def pack_kernel(ids, q_ref, do_ref, o_ref, *outs):
    ones = jnp.ones((EXTRA, HD), bf16)
    for k, out in enumerate(outs):

        @pl.when(pl.program_id(0) == k)
        def _():
            out[0:TOK, 0:WIDE] = q_ref[...]
            out[0:TOK, WIDE : 2 * WIDE] = do_ref[...]
            for h in range(GROUP):
                cols = slice(h * HD, (h + 1) * HD)
                product = do_ref[:, cols].astype(f32) * o_ref[:, cols].astype(f32)
                hi = product.astype(bf16)
                lo = (product - hi.astype(f32)).astype(bf16)
                delta = [
                    lax.dot_general(ones, x, (((1,), (1,)), ((), ())), preferred_element_type=f32) for x in (hi, lo)
                ]
                out[TOK : TOK + EXTRA, cols] = rows_of(delta[0] + delta[1])
            out[TOK : TOK + EXTRA, WIDE : 2 * WIDE] = jnp.zeros((EXTRA, WIDE), bf16)


def pack_rows(ids, *args):
    pack = (TOK + EXTRA, 2 * WIDE)
    rows = pl.BlockSpec((TOK, WIDE), lambda k, ids: (0, lax.rem(ids[0] + k, 4)))
    return pl.pallas_call(
        pack_kernel,
        out_shape=[pltpu.HBM(pack, bf16)] * 4,
        grid_spec=pltpu.PrefetchScalarGridSpec(
            num_scalar_prefetch=1,
            grid=(4,),
            in_specs=[rows] * 3,
            out_specs=[pl.BlockSpec(pack, lambda k, ids: (0, 0))] * 4,
        ),
        compiler_params=pltpu.CompilerParams(vmem_limit_bytes=16 * 2**20),
        name="pack_rows",
    )(ids, *map(in_hbm, args))


def copies_kernel(ids, r1, r2, r3, pair_ref, out_ref):
    for x in range(4):
        for k, ref in enumerate((pair_ref, r1, r2, r3)):
            out_ref[x, k] = ref[...]


def place_of(ids, b):
    far = lax.rem(lax.div(b, 8) - lax.div(ids[1], 8) + 4, 4)
    return lax.rem(b, 4), far, lax.rem(lax.div(b, 4) + lax.div(ids[1], 4), 2)


def attn_kernel(count, B, T, *refs):
    ids, own, other = refs[:3]
    packs, dqs = refs[3 : 3 + count], refs[4 + count : 4 + 2 * count]
    keep, send, ks, vs, kt, qs, dos, delta, p_s, dq_s, dk, dv = refs[4 + 2 * count :]
    c, core = ids[1], ids[2]

    def fill(out, ref):
        def one(b, _):
            out[pl.ds(pl.multiple_of(b * TOK, TOK), TOK), :] = ref[place_of(ids, b)]
            return 0

        lax.fori_loop(0, BLOCKS, one, 0)

    @pl.when(core == 0)
    def _():
        fill(ks, own)
        fill(vs, other)

    @pl.when(core != 0)
    def _():
        fill(ks, other)
        fill(vs, own)

    for r in range(0, ks.shape[0], 512):
        kt[:, r : r + 512] = ks[r : r + 512, :].T
    for i in range(count):
        for h in range(GROUP):
            r = (i * GROUP + h) * TOK
            qs[r : r + TOK, :] = packs[i][0:TOK, h * HD : (h + 1) * HD]
            dos[r : r + TOK, :] = packs[i][0:TOK, (GROUP + h) * HD : (GROUP + h + 1) * HD]
        d = packs[i][TOK : TOK + EXTRA, 0:WIDE].astype(f32)
        delta[0:1, i * WIDE : (i + 1) * WIDE] = d[0:1] + d[1:2] + d[2:3]
    dk[...] = jnp.zeros_like(dk)
    dv[...] = jnp.zeros_like(dv)
    turned = c + 8 * (3 - 2 * lax.div(c, 8))

    def tile(t, _):
        at = jnp.where(t < count // 2, turned, c)
        blocks = lax.div(at * TOK + TOK + B - 1, B)
        t0 = pl.multiple_of(t * T, T)
        q = qs[pl.ds(t0, T), :]
        do = dos[pl.ds(t0, T), :]
        dl = delta[0:1, pl.ds(t0, T)]

        def scores(j, m, masked):
            j0 = pl.multiple_of(j * B, B)
            s = lax.dot_general(ks[pl.ds(j0, B), :], q, (((1,), (1,)), ((), ())), preferred_element_type=f32)
            s = s * (SCALE * LOG2E)
            if masked:
                key = j0 + lax.broadcasted_iota(jnp.int32, (B, T), 0)
                row = at * TOK + (lax.broadcasted_iota(jnp.int32, (B, T), 1) & (TOK - 1))
                s = jnp.where(key <= row, s, -jnp.inf)
            p_s[pl.ds(j0, B), :] = s
            return jnp.maximum(m, jnp.max(s, axis=0, keepdims=True))

        m = jnp.full((1, T), -jnp.inf, f32)
        m = lax.fori_loop(0, blocks - 1, lambda j, m: scores(j, m, False), m)
        m = scores(blocks - 1, m, True)

        def exponents(j, total):
            rows = pl.ds(pl.multiple_of(j * B, B), B)
            e = jnp.exp2(p_s[rows, :] - m)
            p_s[rows, :] = e
            return total + jnp.sum(e, axis=0, keepdims=True)

        inverse = 1.0 / lax.fori_loop(0, blocks, exponents, jnp.zeros((1, T), f32))
        dq_s[...] = jnp.zeros_like(dq_s)

        def backward(j, _):
            j0 = pl.multiple_of(j * B, B)
            rows = pl.ds(j0, B)
            w = p_s[rows, :] * inverse
            dp = lax.dot_general(vs[rows, :], do, (((1,), (1,)), ((), ())), preferred_element_type=f32)
            ds = (w * (dp - dl)).astype(bf16)
            dv[rows, :] += jnp.dot(w.astype(bf16), do, preferred_element_type=f32).astype(bf16).astype(f32)
            part = jnp.dot(ds, q, preferred_element_type=f32) * SCALE
            dk[rows, :] += part.astype(bf16).astype(f32)
            dq_s[...] += jnp.dot(kt[:, rows], ds, preferred_element_type=f32)
            return 0

        lax.fori_loop(0, blocks, backward, 0)
        for r in range(0, T, TOK):
            qs[pl.ds(t0 + r, TOK), :] = (dq_s[:, r : r + TOK].T * SCALE).astype(bf16)
        return 0

    lax.fori_loop(0, count * WIDE // T, tile, 0)
    for i in range(count):
        for h in range(GROUP):
            r = (i * GROUP + h) * TOK
            dqs[i][:, h * HD : (h + 1) * HD] = qs[r : r + TOK, :]

    @pl.when(core == 0)
    def _():
        keep[...] = dk[...]
        send[...] = dv[...].astype(bf16)

    @pl.when(core != 0)
    def _():
        keep[...] = dv[...]
        send[...] = dk[...].astype(bf16)


def attention(ids, own, other, packs, token, B=1024, T=WIDE):
    count, length, rows = len(packs), BLOCKS * TOK, len(packs) * WIDE
    got = call(
        functools.partial(attn_kernel, count, B, T),
        [((TOK, WIDE), bf16)] * count + [((length, HD), f32), ((length, HD), bf16)],
        [ids, own, other, *packs, token],
        "attention",
        1 + count,
        [
            pltpu.VMEM((length, HD), bf16),
            pltpu.VMEM((length, HD), bf16),
            pltpu.VMEM((HD, length), bf16),
            pltpu.VMEM((rows, HD), bf16),
            pltpu.VMEM((rows, HD), bf16),
            pltpu.VMEM((8, rows), f32),
            pltpu.VMEM((length, T), f32),
            pltpu.VMEM((HD, T), f32),
            pltpu.VMEM((length, HD), f32),
            pltpu.VMEM((length, HD), f32),
        ],
        limit=44,
        flops=10 * rows * length * HD,
        nbytes=12 * length * HD,
        free=(count, count + 1),
    )
    return got[:count], got[count:]


def retain_kernel(ids, all_ref, tables, v_ref, out_ref, totals_ref):
    def step(b, state):
        added = all_ref[(*place_of(ids, b), slice(TOK, TOK + HD))]
        return jnp.exp(totals_ref[pl.ds(b, 1), :]) * state + added.astype(f32)

    for b in range(BLOCKS):
        parts = all_ref[(*place_of(ids, jnp.int32(b)), slice(TOK + HD, None))]
        totals_ref[b : b + 1, :] = jnp.sum(parts.astype(f32), axis=0, keepdims=True)
    state = lax.fori_loop(0, ids[1], step, jnp.zeros((HD, HD), f32))
    q, cum, inner = tables[0], tables[2], tables[4]
    out_ref[0] = state
    out_ref[1] = jnp.exp(cum[TOK - 1 : TOK, :]) * state + tables[5]
    out_ref[2] = dot(inner, v_ref[...].astype(f32), 1, 0) + dot(q * jnp.exp(cum), state, 1, 0)


def norm_kernel(ids, parts_ref, states, tables, out_ref, carry_ref):
    def add(i, total):
        return total + parts_ref[i].astype(f32)

    upstream = lax.fori_loop(1, BLOCKS, add, parts_ref[0].astype(f32))
    retained = states[2]
    inverse = lax.rsqrt(jnp.mean(retained * retained, axis=1, keepdims=True) + 1e-06)
    normed = retained * inverse
    grad = (upstream - normed * jnp.mean(normed * upstream, axis=1, keepdims=True)) * inverse
    out_ref[...] = grad
    carry_ref[...] = dot(tables[0] * jnp.exp(tables[2]), grad, 0, 0)


def decay_over(totals, low, high):
    add = lambda m, total: total + totals[pl.ds(m, 1), :]
    return jnp.exp(lax.fori_loop(low, high, add, jnp.zeros((1, HD), f32)))


def scan_x_kernel(ids, r1, r2, r3, carry_ref, totals, group_ref, out_ref, held):
    c = ids[1]
    x = lax.rem(c, 4)
    for k, ref in enumerate((carry_ref, r1, r2, r3)):
        held[k] = ref[...]

    def step(i, grad):
        m = 3 - i
        return held[lax.rem(m - x + 4, 4)] + jnp.exp(totals[pl.ds(c - x + m, 1), :]) * grad

    zero = jnp.zeros((HD, HD), f32)
    group_ref[...] = lax.fori_loop(0, 4, step, zero)
    out_ref[...] = lax.fori_loop(0, 3 - x, step, zero)


def scan_z_kernel(ids, theirs_ref, mine_ref, leaving_ref, totals, both_ref, out_ref):
    c = ids[1]
    first = lax.rem(lax.div(c, 4), 2) == 0
    start = lax.div(c, 8) * 8
    theirs, mine = theirs_ref[...], mine_ref[...]
    low, high = jnp.where(first, mine, theirs), jnp.where(first, theirs, mine)
    both_ref[...] = low + decay_over(totals, start, start + 4) * high
    out_ref[...] = leaving_ref[...] + jnp.where(first, decay_over(totals, c + 1, start + 4) * theirs, 0.0)


def grads_kernel(
    ids, r1, r2, r3, leaving_ref, totals, grad_ref, states, tables, v_ref, dv_ref, part_ref, held
):
    c = ids[1]
    y = lax.div(c, 8)
    for k, ref in enumerate((r1, r2, r3)):
        held[k] = ref[...]

    def step(i, later):
        m = 3 - i
        return held[m - y - 1] + decay_over(totals, m * 8, m * 8 + 8) * later

    later = lax.fori_loop(0, 3 - y, step, jnp.zeros((HD, HD), f32))
    leaving = leaving_ref[...] + decay_over(totals, c + 1, y * 8 + 8) * later
    grad, state = grad_ref[...], states[0]
    q, k, cum, decay, inner = (tables[i] for i in range(5))
    v = v_ref[...].astype(f32)
    total = cum[TOK - 1 : TOK, :]
    tail = jnp.exp(total - cum)
    pair = decay * dot(grad, v, 1, 1)
    dq = jnp.exp(cum) * dot(grad, state, 1, 1) + dot(pair, k, 1, 0)
    dk = dot(pair, q, 0, 0) + tail * dot(v, leaving, 1, 1)
    dv_ref[...] = dot(inner, grad, 0, 0) + tail * dot(k, leaving, 1, 0)
    through = jnp.sum(jnp.sum(leaving * states[1], axis=1, keepdims=True), axis=0, keepdims=True)
    change = jnp.sum(grad * states[2], axis=1, keepdims=True) - jnp.sum(k * dk, axis=1, keepdims=True)
    t = lax.broadcasted_iota(jnp.int32, (TOK, TOK), 0)
    s = lax.broadcasted_iota(jnp.int32, (TOK, TOK), 1)
    da = dot(jnp.broadcast_to(change, (TOK, HD)), (s <= t).astype(f32), 0, 0) + through
    part_ref[0:TOK, 0:HD] = dq * SCALE
    part_ref[0:TOK, HD : 2 * HD] = dk
    part_ref[TOK : TOK + EXTRA, 0:HD] = da[0:EXTRA]
    part_ref[TOK : TOK + EXTRA, HD : 2 * HD] = jnp.zeros((EXTRA, HD), f32)


def message_kernel(ids, a_ref, b_ref, out_ref):
    out_ref[0:TOK, :] = (a_ref[0:TOK, :] + b_ref[0:TOK, :]).astype(bf16)
    tail = slice(TOK, TOK + EXTRA)
    hi, mid, lo = thirds(a_ref[tail, :] + b_ref[tail, :])
    row = lax.broadcasted_iota(jnp.int32, hi.shape, 0)
    parts = jnp.where(row == 0, hi, jnp.where(row == 1, mid, jnp.where(row == 2, lo, 0.0)))
    out_ref[tail, :] = parts.astype(bf16)


def finish_kernel(ids, *refs):
    messages, (dq_ref, dk_ref, da_ref) = refs[:4], refs[4:]
    row = lax.broadcasted_iota(jnp.int32, da_ref.shape, 0)
    da = jnp.zeros(da_ref.shape, f32)
    for k, ref in enumerate(messages):
        head = lax.rem(ids[0] + 3 - k, 4)
        cols = pl.ds(pl.multiple_of(head * HD, HD), HD)
        dq_ref[:, cols] = ref[0:TOK, 0:HD].astype(f32)
        dk_ref[:, cols] = ref[0:TOK, HD : 2 * HD].astype(f32)
        value = jnp.sum(ref[TOK : TOK + EXTRA, 0:HD].astype(f32), axis=0, keepdims=True)
        da = jnp.where(row == head, value, da)
    da_ref[...] = da


def rows_kernel(ids, *refs):
    parts, out = refs[:4], refs[4]
    for k, ref in enumerate(parts):
        start = pl.multiple_of(lax.rem(ids[0] + 1 + k, 4) * WIDE, HD)
        out[:, pl.ds(start, WIDE)] = ref[...]


def arrival(arrays):
    def kernel(*refs):
        copy = pltpu.make_async_copy(refs[0].at[0:EXTRA, 0:HD], refs[-2], refs[-1])
        copy.start()
        copy.wait()

    return pl.pallas_call(
        kernel,
        out_shape=jax.ShapeDtypeStruct((EXTRA, HD), bf16),
        in_specs=[ANY] * len(arrays),
        out_specs=VMEM,
        scratch_shapes=[pltpu.SemaphoreType.DMA],
        cost_estimate=pl.CostEstimate(flops=5 * 10**10, bytes_accessed=0, transcendentals=0),
        name="arrival",
    )(*arrays)


def shift(x, k, turn=False):
    if not turn:
        return lax.ppermute(x, "zhi", [(i, (i + k) % 4) for i in range(4)])
    pairs = [(4 * i + y, (i + k) % 4 * 4 + 3 - y) for i in range(4) for y in range(4)]
    return lax.ppermute(x, ("zhi", "y"), pairs)


def from_next(x, axis, k):
    return lax.ppermute(x, axis, [(i, (i - k) % 4) for i in range(4)])


def swap(x):
    return lax.ppermute(x, "core", [(0, 1), (1, 0)])


def spread(x):
    return lax.all_to_all(x, CTX, 0, 0)


def on_device(queries, attn_out, grad_out, shared_kv, ret_query, ret_key, ret_value, log_decay):
    z = lax.axis_index("zhi")
    ids = jnp.stack([z, lax.axis_index(CTX), lax.axis_index("core")]).astype(jnp.int32)
    mine, tables = call(
        local_kernel,
        [((TOK + HD + EXTRA, HD), bf16), ((6, TOK, HD), f32)],
        [ids, shared_kv, ret_query, ret_key, ret_value, log_decay.T],
        "retention_local",
        free=(0,),
    )
    packs = pack_rows(ids, queries[0], grad_out[0], attn_out[0])
    theirs = lax.ppermute(mine, "zlo", [(0, 1), (1, 0)])
    theirs, packs = lax.optimization_barrier((theirs, packs))
    pair = jnp.stack([mine, theirs])
    near = [from_next(pair, "y", k) for k in (1, 2, 3)]
    near, packs = lax.optimization_barrier((near, packs))
    from1, from3, from2 = shift(packs[1], 1, True), shift(packs[3], 3, True), shift(packs[2], 2)
    (copies,) = call(copies_kernel, [((4, 4, *pair.shape), bf16)], [ids, *near, pair], "copies", 4)
    blocks = lax.all_to_all(copies, "x", 0, 0)
    own = blocks[:, :, :, 0:TOK]
    own, token = lax.optimization_barrier((own, arrival([from1, from3, from2])))
    other = swap(own)
    (dq1, dq3, dq2, dq0), (keep, send) = attention(ids, own, other, [from1, from3, from2, packs[0]], token)
    back1, back3, back2 = shift(dq1, 3, True), shift(dq3, 1, True), shift(dq2, 2)

    square = ((TOK, HD), f32)
    states, totals = call(
        retain_kernel, [((3, TOK, HD), f32), ((BLOCKS, HD), f32)], [ids, blocks, tables, ret_value], "retention_forward", 1
    )
    part = (keep + swap(send).astype(f32)).astype(bf16)
    parts = spread(part.reshape(BLOCKS, TOK, HD))
    parts, back2 = lax.optimization_barrier((parts, back2))
    grad, carry = call(
        norm_kernel, [square] * 2, [ids, parts, states, tables], "norm_backward", 1, free=(1,)
    )
    held = pltpu.VMEM((4, HD, HD), f32)
    near = [from_next(carry, "x", k) for k in (1, 2, 3)]
    group, leaving = call(scan_x_kernel, [square] * 2, [ids, *near, carry, totals], "scan_x", 4, [held], free=(0, 1))
    theirs = lax.ppermute(group, "zlo", [(0, 1), (1, 0)])
    both, leaving = call(scan_z_kernel, [square] * 2, [ids, theirs, group, leaving, totals], "scan_z", 3, free=(0, 1))
    far = [from_next(both, "y", k) for k in (1, 2, 3)]
    *far, back1, back3 = lax.optimization_barrier((*far, back1, back3))
    d_value, half = call(
        grads_kernel,
        [square, ((TOK + EXTRA, 2 * HD), f32)],
        [ids, *far, leaving, totals, grad, states, tables, ret_value],
        "retention_grads",
        4,
        [held],
        free=(1,),
    )
    (message,) = call(
        message_kernel, [((TOK + EXTRA, 2 * HD), bf16)], [ids, swap(half), half], "message", 2, free=(0,)
    )
    d_query, d_key, d_decay = call(
        finish_kernel,
        [(ret_query.shape, f32), (ret_key.shape, f32), (log_decay.shape[::-1], f32)],
        [ids, *(shift(message, k) for k in (1, 2, 3)), message],
        "finish",
        4,
    )
    (d_queries,) = call(
        rows_kernel, [((TOK, 4 * WIDE), bf16)], [ids, back1, back2, back3, dq0], "query_rows", 3
    )
    return d_queries[None], d_query, d_key, d_value, d_decay.T


def solution(mesh):
    fine = Mesh(mesh.devices.reshape(4, 2, 4, 2, 4), ("zhi", "core", "y", "zlo", "x"))
    section = ("zhi", "core")
    rows = P(section, CTX, None)
    return jax.shard_map(
        on_device,
        mesh=fine,
        in_specs=(rows, rows, rows, P(CTX, section), P(CTX, None), P(CTX, None), P(CTX, section), P(CTX, None)),
        out_specs=(rows, P(CTX, None), P(CTX, None), P(CTX, section), P(CTX, None)),
        check_vma=False,
    )
```

```python
import functools
import math

import jax
import jax.numpy as jnp
from jax import lax
from jax.experimental import pallas as pl
from jax.experimental.pallas import tpu as pltpu
from jax.sharding import Mesh, PartitionSpec as P

bf16 = jnp.bfloat16
f32 = jnp.float32
EXACT = lax.Precision.HIGHEST
TOK = 128
HD = 128
GROUP = 5
WIDE = GROUP * HD
EXTRA = 16
BLOCKS = 32
SCALE = HD**-0.5
LOG2E = math.log2(math.e)
CTX = ("y", "zlo", "x")
VMEM = pl.BlockSpec(memory_space=pltpu.VMEM)
SMEM = pl.BlockSpec(memory_space=pltpu.SMEM)


ANY = pl.BlockSpec(memory_space=pl.ANY)


def in_hbm(x):
    return pltpu.with_memory_space_constraint(x, pltpu.HBM)


def loaded(kernel, inputs, outputs, *refs):
    ids, far, rest = refs[0], refs[1 : 1 + inputs], refs[1 + inputs :]
    results, near, scratch = rest[:outputs], rest[outputs : outputs + inputs], rest[outputs + inputs : -1]
    copies = [pltpu.make_async_copy(f, n, rest[-1].at[i]) for i, (f, n) in enumerate(zip(far, near))]
    for copy in copies:
        copy.start()
    for copy in copies:
        copy.wait()
    kernel(ids, *near, *results, *scratch)


def call(kernel, outs, args, name, loose=0, scratch=(), limit=8, flops=0, nbytes=0, free=()):
    cost = None
    if flops:
        cost = pl.CostEstimate(flops=flops, bytes_accessed=nbytes, transcendentals=0)
    inputs = [x if i < loose else in_hbm(x) for i, x in enumerate(args[1:])]
    near = [pltpu.VMEM(x.shape, x.dtype) for x in inputs]
    return pl.pallas_call(
        functools.partial(loaded, kernel, len(inputs), len(outs)),
        out_shape=[jax.ShapeDtypeStruct(s, t) if i in free else pltpu.HBM(s, t) for i, (s, t) in enumerate(outs)],
        in_specs=[SMEM] + [ANY] * len(inputs),
        out_specs=[VMEM] * len(outs),
        scratch_shapes=near + list(scratch) + [pltpu.SemaphoreType.DMA((len(inputs),))],
        compiler_params=pltpu.CompilerParams(vmem_limit_bytes=limit * 2**20),
        cost_estimate=cost,
        name=name,
    )(args[0], *inputs)


def dot(a, b, ca, cb):
    return lax.dot_general(a, b, (((ca,), (cb,)), ((), ())), precision=EXACT, preferred_element_type=f32)


def thirds(x):
    hi = x.astype(bf16).astype(f32)
    mid = (x - hi).astype(bf16).astype(f32)
    return hi, mid, x - hi - mid


def rows_of(x):
    row = lax.broadcasted_iota(jnp.int32, x.shape, 0)
    hi, mid, lo = thirds(x)
    return jnp.where(row == 0, hi, jnp.where(row == 1, mid, jnp.where(row == 2, lo, 0.0))).astype(bf16)


def local_kernel(ids, kv_ref, rq_ref, rk_ref, rv_ref, a_ref, mine, tables):
    head = ids[0]
    cols = pl.ds(pl.multiple_of(head * HD, HD), HD)
    q = rq_ref[:, cols].astype(f32) * SCALE
    k = rk_ref[:, cols].astype(f32)
    v = rv_ref[...].astype(f32)
    pick = lax.broadcasted_iota(jnp.int32, a_ref.shape, 0) == head
    a = jnp.sum(jnp.where(pick, a_ref[...], 0.0), axis=0, keepdims=True)
    a = jnp.broadcast_to(a, (HD, TOK))
    t = lax.broadcasted_iota(jnp.int32, (TOK, TOK), 0)
    s = lax.broadcasted_iota(jnp.int32, (TOK, TOK), 1)
    cum = dot((s <= t).astype(f32), a, 1, 1)
    across = dot(a, (t <= s).astype(f32), 1, 0)
    decay = jnp.exp(jnp.where(s <= t, cum - across, -jnp.inf))
    total = cum[TOK - 1 : TOK, :]
    state = dot(k * jnp.exp(total - cum), v, 0, 0)
    mine[0:TOK, :] = kv_ref[...]
    mine[TOK : TOK + HD, :] = state.astype(bf16)
    mine[TOK + HD :, :] = rows_of(jnp.broadcast_to(total, (EXTRA, HD)))
    tables[0] = q
    tables[1] = k
    tables[2] = cum
    tables[3] = decay
    tables[4] = decay * dot(q, k, 1, 1)
    tables[5] = state


def pack_kernel(ids, q_ref, do_ref, o_ref, *outs):
    ones = jnp.ones((EXTRA, HD), bf16)
    for k, out in enumerate(outs):

        @pl.when(pl.program_id(0) == k)
        def _():
            out[0:TOK, 0:WIDE] = q_ref[...]
            out[0:TOK, WIDE : 2 * WIDE] = do_ref[...]
            for h in range(GROUP):
                cols = slice(h * HD, (h + 1) * HD)
                product = do_ref[:, cols].astype(f32) * o_ref[:, cols].astype(f32)
                hi = product.astype(bf16)
                lo = (product - hi.astype(f32)).astype(bf16)
                delta = [
                    lax.dot_general(ones, x, (((1,), (1,)), ((), ())), preferred_element_type=f32) for x in (hi, lo)
                ]
                out[TOK : TOK + EXTRA, cols] = rows_of(delta[0] + delta[1])
            out[TOK : TOK + EXTRA, WIDE : 2 * WIDE] = jnp.zeros((EXTRA, WIDE), bf16)


def pack_rows(ids, *args):
    pack = (TOK + EXTRA, 2 * WIDE)
    rows = pl.BlockSpec((TOK, WIDE), lambda k, ids: (0, lax.rem(ids[0] + k, 4)))
    return pl.pallas_call(
        pack_kernel,
        out_shape=[pltpu.HBM(pack, bf16)] * 4,
        grid_spec=pltpu.PrefetchScalarGridSpec(
            num_scalar_prefetch=1,
            grid=(4,),
            in_specs=[rows] * 3,
            out_specs=[pl.BlockSpec(pack, lambda k, ids: (0, 0))] * 4,
        ),
        compiler_params=pltpu.CompilerParams(vmem_limit_bytes=16 * 2**20),
        name="pack_rows",
    )(ids, *map(in_hbm, args))


def copies_kernel(ids, r1, r2, r3, pair_ref, out_ref):
    for x in range(4):
        for k, ref in enumerate((pair_ref, r1, r2, r3)):
            out_ref[x, k] = ref[...]


def place_of(ids, b):
    far = lax.rem(lax.div(b, 8) - lax.div(ids[1], 8) + 4, 4)
    return lax.rem(b, 4), far, lax.rem(lax.div(b, 4) + lax.div(ids[1], 4), 2)


def attn_kernel(count, B, T, *refs):
    ids, own, other = refs[:3]
    packs, dqs = refs[3 : 3 + count], refs[4 + count : 4 + 2 * count]
    keep, send, ks, vs, kt, qs, dos, delta, p_s, dq_s, dk, dv = refs[4 + 2 * count :]
    c, core = ids[1], ids[2]

    def fill(out, ref):
        def one(b, _):
            out[pl.ds(pl.multiple_of(b * TOK, TOK), TOK), :] = ref[place_of(ids, b)]
            return 0

        lax.fori_loop(0, BLOCKS, one, 0)

    @pl.when(core == 0)
    def _():
        fill(ks, own)
        fill(vs, other)

    @pl.when(core != 0)
    def _():
        fill(ks, other)
        fill(vs, own)

    for r in range(0, ks.shape[0], 512):
        kt[:, r : r + 512] = ks[r : r + 512, :].T
    for i in range(count):
        for h in range(GROUP):
            r = (i * GROUP + h) * TOK
            qs[r : r + TOK, :] = packs[i][0:TOK, h * HD : (h + 1) * HD]
            dos[r : r + TOK, :] = packs[i][0:TOK, (GROUP + h) * HD : (GROUP + h + 1) * HD]
        d = packs[i][TOK : TOK + EXTRA, 0:WIDE].astype(f32)
        delta[0:1, i * WIDE : (i + 1) * WIDE] = d[0:1] + d[1:2] + d[2:3]
    dk[...] = jnp.zeros_like(dk)
    dv[...] = jnp.zeros_like(dv)
    turned = c + 8 * (3 - 2 * lax.div(c, 8))

    def tile(t, _):
        at = jnp.where(t < count // 2, turned, c)
        blocks = lax.div(at * TOK + TOK + B - 1, B)
        t0 = pl.multiple_of(t * T, T)
        q = qs[pl.ds(t0, T), :]
        do = dos[pl.ds(t0, T), :]
        dl = delta[0:1, pl.ds(t0, T)]

        def scores(j, m, masked):
            j0 = pl.multiple_of(j * B, B)
            s = lax.dot_general(ks[pl.ds(j0, B), :], q, (((1,), (1,)), ((), ())), preferred_element_type=f32)
            s = s * (SCALE * LOG2E)
            if masked:
                key = j0 + lax.broadcasted_iota(jnp.int32, (B, T), 0)
                row = at * TOK + (lax.broadcasted_iota(jnp.int32, (B, T), 1) & (TOK - 1))
                s = jnp.where(key <= row, s, -jnp.inf)
            p_s[pl.ds(j0, B), :] = s
            return jnp.maximum(m, jnp.max(s, axis=0, keepdims=True))

        m = jnp.full((1, T), -jnp.inf, f32)
        m = lax.fori_loop(0, blocks - 1, lambda j, m: scores(j, m, False), m)
        m = scores(blocks - 1, m, True)

        def exponents(j, total):
            rows = pl.ds(pl.multiple_of(j * B, B), B)
            e = jnp.exp2(p_s[rows, :] - m)
            p_s[rows, :] = e
            return total + jnp.sum(e, axis=0, keepdims=True)

        inverse = 1.0 / lax.fori_loop(0, blocks, exponents, jnp.zeros((1, T), f32))
        dq_s[...] = jnp.zeros_like(dq_s)

        def backward(j, _):
            j0 = pl.multiple_of(j * B, B)
            rows = pl.ds(j0, B)
            w = p_s[rows, :] * inverse
            dp = lax.dot_general(vs[rows, :], do, (((1,), (1,)), ((), ())), preferred_element_type=f32)
            ds = (w * (dp - dl)).astype(bf16)
            dv[rows, :] += jnp.dot(w.astype(bf16), do, preferred_element_type=f32).astype(bf16).astype(f32)
            part = jnp.dot(ds, q, preferred_element_type=f32) * SCALE
            dk[rows, :] += part.astype(bf16).astype(f32)
            dq_s[...] += jnp.dot(kt[:, rows], ds, preferred_element_type=f32)
            return 0

        lax.fori_loop(0, blocks, backward, 0)
        for r in range(0, T, TOK):
            qs[pl.ds(t0 + r, TOK), :] = (dq_s[:, r : r + TOK].T * SCALE).astype(bf16)
        return 0

    lax.fori_loop(0, count * WIDE // T, tile, 0)
    for i in range(count):
        for h in range(GROUP):
            r = (i * GROUP + h) * TOK
            dqs[i][:, h * HD : (h + 1) * HD] = qs[r : r + TOK, :]

    @pl.when(core == 0)
    def _():
        keep[...] = dk[...]
        send[...] = dv[...].astype(bf16)

    @pl.when(core != 0)
    def _():
        keep[...] = dv[...]
        send[...] = dk[...].astype(bf16)


def attention(ids, own, other, packs, token, B=1024, T=WIDE):
    count, length, rows = len(packs), BLOCKS * TOK, len(packs) * WIDE
    got = call(
        functools.partial(attn_kernel, count, B, T),
        [((TOK, WIDE), bf16)] * count + [((length, HD), f32), ((length, HD), bf16)],
        [ids, own, other, *packs, token],
        "attention",
        1 + count,
        [
            pltpu.VMEM((length, HD), bf16),
            pltpu.VMEM((length, HD), bf16),
            pltpu.VMEM((HD, length), bf16),
            pltpu.VMEM((rows, HD), bf16),
            pltpu.VMEM((rows, HD), bf16),
            pltpu.VMEM((8, rows), f32),
            pltpu.VMEM((length, T), f32),
            pltpu.VMEM((HD, T), f32),
            pltpu.VMEM((length, HD), f32),
            pltpu.VMEM((length, HD), f32),
        ],
        limit=44,
        flops=10 * rows * length * HD,
        nbytes=12 * length * HD,
        free=(count, count + 1),
    )
    return got[:count], got[count:]


def retain_kernel(ids, all_ref, tables, v_ref, out_ref, totals_ref):
    def step(b, state):
        added = all_ref[(*place_of(ids, b), slice(TOK, TOK + HD))]
        return jnp.exp(totals_ref[pl.ds(b, 1), :]) * state + added.astype(f32)

    for b in range(BLOCKS):
        parts = all_ref[(*place_of(ids, jnp.int32(b)), slice(TOK + HD, None))]
        totals_ref[b : b + 1, :] = jnp.sum(parts.astype(f32), axis=0, keepdims=True)
    state = lax.fori_loop(0, ids[1], step, jnp.zeros((HD, HD), f32))
    q, cum, inner = tables[0], tables[2], tables[4]
    out_ref[0] = state
    out_ref[1] = jnp.exp(cum[TOK - 1 : TOK, :]) * state + tables[5]
    out_ref[2] = dot(inner, v_ref[...].astype(f32), 1, 0) + dot(q * jnp.exp(cum), state, 1, 0)


def norm_kernel(ids, parts_ref, states, tables, out_ref, carry_ref):
    def add(i, total):
        return total + parts_ref[i].astype(f32)

    upstream = lax.fori_loop(1, BLOCKS, add, parts_ref[0].astype(f32))
    retained = states[2]
    inverse = lax.rsqrt(jnp.mean(retained * retained, axis=1, keepdims=True) + 1e-06)
    normed = retained * inverse
    grad = (upstream - normed * jnp.mean(normed * upstream, axis=1, keepdims=True)) * inverse
    out_ref[...] = grad
    carry_ref[...] = dot(tables[0] * jnp.exp(tables[2]), grad, 0, 0)


def decay_over(totals, low, high):
    add = lambda m, total: total + totals[pl.ds(m, 1), :]
    return jnp.exp(lax.fori_loop(low, high, add, jnp.zeros((1, HD), f32)))


def scan_x_kernel(ids, r1, r2, r3, carry_ref, totals, group_ref, out_ref, held):
    c = ids[1]
    x = lax.rem(c, 4)
    for k, ref in enumerate((carry_ref, r1, r2, r3)):
        held[k] = ref[...]

    def step(i, grad):
        m = 3 - i
        return held[lax.rem(m - x + 4, 4)] + jnp.exp(totals[pl.ds(c - x + m, 1), :]) * grad

    zero = jnp.zeros((HD, HD), f32)
    group_ref[...] = lax.fori_loop(0, 4, step, zero)
    out_ref[...] = lax.fori_loop(0, 3 - x, step, zero)


def scan_z_kernel(ids, theirs_ref, mine_ref, leaving_ref, totals, both_ref, out_ref):
    c = ids[1]
    first = lax.rem(lax.div(c, 4), 2) == 0
    start = lax.div(c, 8) * 8
    theirs, mine = theirs_ref[...], mine_ref[...]
    low, high = jnp.where(first, mine, theirs), jnp.where(first, theirs, mine)
    both_ref[...] = low + decay_over(totals, start, start + 4) * high
    out_ref[...] = leaving_ref[...] + jnp.where(first, decay_over(totals, c + 1, start + 4) * theirs, 0.0)


def near_kernel(ids, grad_ref, states, tables, v_ref, out_ref):
    grad, state = grad_ref[...], states[0]
    q, k, cum, decay, inner = (tables[i] for i in range(5))
    pair = decay * dot(grad, v_ref[...].astype(f32), 1, 1)
    out_ref[0] = (jnp.exp(cum) * dot(grad, state, 1, 1) + dot(pair, k, 1, 0)) * SCALE
    out_ref[1] = dot(pair, q, 0, 0)
    out_ref[2] = dot(inner, grad, 0, 0)
    out_ref[3] = jnp.broadcast_to(jnp.sum(grad * states[2], axis=1, keepdims=True), (TOK, HD))


def grads_kernel(ids, r1, r2, r3, leaving_ref, near_ref, totals, states, tables, v_ref, dv_ref, part_ref, held):
    c = ids[1]
    y = lax.div(c, 8)
    for k, ref in enumerate((r1, r2, r3)):
        held[k] = ref[...]

    def step(i, later):
        m = 3 - i
        return held[m - y - 1] + decay_over(totals, m * 8, m * 8 + 8) * later

    later = lax.fori_loop(0, 3 - y, step, jnp.zeros((HD, HD), f32))
    leaving = leaving_ref[...] + decay_over(totals, c + 1, y * 8 + 8) * later
    k, cum = tables[1], tables[2]
    total = cum[TOK - 1 : TOK, :]
    tail = jnp.exp(total - cum)
    dk = near_ref[1] + tail * dot(v_ref[...].astype(f32), leaving, 1, 1)
    dv_ref[...] = near_ref[2] + tail * dot(k, leaving, 1, 0)
    through = jnp.sum(jnp.sum(leaving * states[1], axis=1, keepdims=True), axis=0, keepdims=True)
    change = near_ref[3] - jnp.sum(k * dk, axis=1, keepdims=True)
    t = lax.broadcasted_iota(jnp.int32, (TOK, TOK), 0)
    s = lax.broadcasted_iota(jnp.int32, (TOK, TOK), 1)
    da = dot(change, (s <= t).astype(f32), 0, 0) + through
    part_ref[0:TOK, 0:HD] = near_ref[0]
    part_ref[0:TOK, HD : 2 * HD] = dk
    part_ref[TOK : TOK + EXTRA, 0:HD] = da[0:EXTRA]
    part_ref[TOK : TOK + EXTRA, HD : 2 * HD] = jnp.zeros((EXTRA, HD), f32)


def message_kernel(ids, a_ref, b_ref, out_ref):
    out_ref[0:TOK, :] = (a_ref[0:TOK, :] + b_ref[0:TOK, :]).astype(bf16)
    tail = slice(TOK, TOK + EXTRA)
    hi, mid, lo = thirds(a_ref[tail, :] + b_ref[tail, :])
    row = lax.broadcasted_iota(jnp.int32, hi.shape, 0)
    parts = jnp.where(row == 0, hi, jnp.where(row == 1, mid, jnp.where(row == 2, lo, 0.0)))
    out_ref[tail, :] = parts.astype(bf16)


def finish_kernel(ids, *refs):
    messages, (dq_ref, dk_ref, da_ref) = refs[:4], refs[4:]
    row = lax.broadcasted_iota(jnp.int32, da_ref.shape, 0)
    da = jnp.zeros(da_ref.shape, f32)
    for k, ref in enumerate(messages):
        head = lax.rem(ids[0] + 3 - k, 4)
        cols = pl.ds(pl.multiple_of(head * HD, HD), HD)
        dq_ref[:, cols] = ref[0:TOK, 0:HD].astype(f32)
        dk_ref[:, cols] = ref[0:TOK, HD : 2 * HD].astype(f32)
        value = jnp.sum(ref[TOK : TOK + EXTRA, 0:HD].astype(f32), axis=0, keepdims=True)
        da = jnp.where(row == head, value, da)
    da_ref[...] = da


def rows_kernel(ids, *refs):
    parts, out = refs[:4], refs[4]
    for k, ref in enumerate(parts):
        start = pl.multiple_of(lax.rem(ids[0] + 1 + k, 4) * WIDE, HD)
        out[:, pl.ds(start, WIDE)] = ref[...]


def arrival(arrays):
    def kernel(*refs):
        copy = pltpu.make_async_copy(refs[0].at[0:EXTRA, 0:HD], refs[-2], refs[-1])
        copy.start()
        copy.wait()

    return pl.pallas_call(
        kernel,
        out_shape=jax.ShapeDtypeStruct((EXTRA, HD), bf16),
        in_specs=[ANY] * len(arrays),
        out_specs=VMEM,
        scratch_shapes=[pltpu.SemaphoreType.DMA],
        cost_estimate=pl.CostEstimate(flops=5 * 10**10, bytes_accessed=0, transcendentals=0),
        name="arrival",
    )(*arrays)


def shift(x, k, turn=False):
    if not turn:
        return lax.ppermute(x, "zhi", [(i, (i + k) % 4) for i in range(4)])
    pairs = [(4 * i + y, (i + k) % 4 * 4 + 3 - y) for i in range(4) for y in range(4)]
    return lax.ppermute(x, ("zhi", "y"), pairs)


def from_next(x, axis, k):
    return lax.ppermute(x, axis, [(i, (i - k) % 4) for i in range(4)])


def swap(x):
    return lax.ppermute(x, "core", [(0, 1), (1, 0)])


def spread(x):
    return lax.all_to_all(x, CTX, 0, 0)


def on_device(queries, attn_out, grad_out, shared_kv, ret_query, ret_key, ret_value, log_decay):
    z = lax.axis_index("zhi")
    ids = jnp.stack([z, lax.axis_index(CTX), lax.axis_index("core")]).astype(jnp.int32)
    mine, tables = call(
        local_kernel,
        [((TOK + HD + EXTRA, HD), bf16), ((6, TOK, HD), f32)],
        [ids, shared_kv, ret_query, ret_key, ret_value, log_decay.T],
        "retention_local",
        free=(0,),
    )
    packs = pack_rows(ids, queries[0], grad_out[0], attn_out[0])
    theirs = lax.ppermute(mine, "zlo", [(0, 1), (1, 0)])
    theirs, packs = lax.optimization_barrier((theirs, packs))
    pair = jnp.stack([mine, theirs])
    near = [from_next(pair, "y", k) for k in (1, 2, 3)]
    near, packs = lax.optimization_barrier((near, packs))
    from1, from3, from2 = shift(packs[1], 1, True), shift(packs[3], 3, True), shift(packs[2], 2)
    (copies,) = call(copies_kernel, [((4, 4, *pair.shape), bf16)], [ids, *near, pair], "copies", 4)
    blocks = lax.all_to_all(copies, "x", 0, 0)
    own = blocks[:, :, :, 0:TOK]
    own, token = lax.optimization_barrier((own, arrival([from1, from3, from2])))
    other = swap(own)
    (dq1, dq3, dq2, dq0), (keep, send) = attention(ids, own, other, [from1, from3, from2, packs[0]], token)
    back1, back3, back2 = shift(dq1, 3, True), shift(dq3, 1, True), shift(dq2, 2)

    square = ((TOK, HD), f32)
    states, totals = call(
        retain_kernel, [((3, TOK, HD), f32), ((BLOCKS, HD), f32)], [ids, blocks, tables, ret_value], "retention_forward", 1
    )
    part = (keep + swap(send).astype(f32)).astype(bf16)
    parts = spread(part.reshape(BLOCKS, TOK, HD))
    parts, back2 = lax.optimization_barrier((parts, back2))
    grad, carry = call(
        norm_kernel, [square] * 2, [ids, parts, states, tables], "norm_backward", 1, free=(1,)
    )
    held = pltpu.VMEM((4, HD, HD), f32)
    (ahead,) = call(
        near_kernel, [((4, TOK, HD), f32)], [ids, grad, states, tables, ret_value], "grads_near", flops=10**9, nbytes=10**6, free=(0,)
    )
    near = [from_next(carry, "x", k) for k in (1, 2, 3)]
    group, leaving = call(scan_x_kernel, [square] * 2, [ids, *near, carry, totals], "scan_x", 4, [held], free=(0, 1))
    theirs = lax.ppermute(group, "zlo", [(0, 1), (1, 0)])
    both, leaving = call(scan_z_kernel, [square] * 2, [ids, theirs, group, leaving, totals], "scan_z", 3, free=(0, 1))
    far = [from_next(both, "y", k) for k in (1, 2, 3)]
    *far, back1, back3 = lax.optimization_barrier((*far, back1, back3))
    d_value, half = call(
        grads_kernel,
        [square, ((TOK + EXTRA, 2 * HD), f32)],
        [ids, *far, leaving, ahead, totals, states, tables, ret_value],
        "retention_grads",
        5,
        [held],
        free=(1,),
    )
    (message,) = call(
        message_kernel, [((TOK + EXTRA, 2 * HD), bf16)], [ids, swap(half), half], "message", 2, free=(0,)
    )
    d_query, d_key, d_decay = call(
        finish_kernel,
        [(ret_query.shape, f32), (ret_key.shape, f32), (log_decay.shape[::-1], f32)],
        [ids, *(shift(message, k) for k in (1, 2, 3)), message],
        "finish",
        4,
    )
    (d_queries,) = call(
        rows_kernel, [((TOK, 4 * WIDE), bf16)], [ids, back1, back2, back3, dq0], "query_rows", 3
    )
    return d_queries[None], d_query, d_key, d_value, d_decay.T


def solution(mesh):
    fine = Mesh(mesh.devices.reshape(4, 2, 4, 2, 4), ("zhi", "core", "y", "zlo", "x"))
    section = ("zhi", "core")
    rows = P(section, CTX, None)
    return jax.shard_map(
        on_device,
        mesh=fine,
        in_specs=(rows, rows, rows, P(CTX, section), P(CTX, None), P(CTX, None), P(CTX, section), P(CTX, None)),
        out_specs=(rows, P(CTX, None), P(CTX, None), P(CTX, section), P(CTX, None)),
        check_vma=False,
    )
```
